256 devices in a mesh: pts: 256 (over y, z, x, core).
Axes of the slice: x: 4, y: 4, z: 8, core: 2. Of those that a mesh axis runs over, the one named last changes fastest.
Arguments:
- vectors: bfloat16 [4096, 8, 256], P('pts'), may hold values from -6 to 6
- leaf_basis: bfloat16 [4096, 64, 256], P('pts'), may hold values from -0.375 to 0.375
- leaf_transfer: bfloat16 [4096, 64, 64], P('pts'), may hold values from -0.1875 to 0.1875
- leaf_coupling: bfloat16 [4096, 64, 384], P('pts'), may hold values from -0.3125 to 0.3125
- near_tiles: bfloat16 [4096, 4, 256, 256], P('pts'), may hold values from -0.1875 to 0.1875
- tile_scale: float32 [4096, 4], P('pts'), may hold values from 0.3 to 3
- near_boxes: int32 [4096, 4], P('pts'), may hold values from 0 to 4095, as said below
- near_counts: int32 [4096], P('pts'), may hold values from 1 to 4, as said below
- far_boxes: int32 [4096, 6], P('pts'), may hold values from 0 to 4095, as said below
- level_up: float32 [256, 5, 64, 64], P('pts'), may hold values from -0.75 to 0.75
- level_coupling: float32 [256, 5, 64, 64], P('pts'), may hold values from -0.3125 to 0.3125
Outputs:
- product: float32 [4096, 8, 256], P('pts')
The draws below stay inside these ranges and needn't reach their ends.
Inputs may be any that keep to these rules, and one draw needn't show every extreme that they name: Slot 0 of row b of near_boxes is b itself; every entry of a row on device d names a box on devices d - 7 to d + 7; all entries of slots 1 and up of near_boxes and all entries of far_boxes in the rows of one device d together name at most 4 distinct boxes of any one other device, and exactly 4 of some other device. `near_counts`: every device has a box with all 4 slots used. `far_boxes`: every entry of a row on device d names a box on devices d - 7 to d + 7.
All inputs are finite; a program needn't handle non-finite values.
Results may differ from the reference program's by a relative error of at most 0.009.
Values may be sent and summed in bfloat16 or wider, within the bound.
No kernel may reach another device: no remote copies, remote signals or barrier semaphores. Data moves between devices by JAX's collectives and lax.ppermute only.
A program may use at most 64 MiB of HBM per device.

```python
import math
import jax
import jax.numpy as jnp
from jax import lax

LEAF = 256
RANK = 64
RHS = 8
NEAR = 4
FAR = 6
UP = 5
BOX_DEV = 16
REACH = 7
SEL = 4
NBOX = 4096
N_PTS = 256


def box_picks(key):
    devices = NBOX // BOX_DEV
    picks_key = jax.random.fold_in(key, 21)
    scores = jax.random.randint(picks_key, (devices, 2 * REACH + 1, BOX_DEV), 0, 2 ** 20)
    scores = scores * BOX_DEV + jnp.arange(BOX_DEV, dtype=jnp.int32)[None, None, :]
    order = jnp.argsort(scores, axis=2, stable=True).astype(jnp.int32)
    return order[:, :, :SEL]


def pick_boxes(key, slots):
    devices = NBOX // BOX_DEV
    key_offset, key_within = jax.random.split(key)
    own_box = jnp.arange(NBOX, dtype=jnp.int32)
    home_dev = own_box // BOX_DEV
    offset = jax.random.randint(key_offset, (NBOX, slots), -REACH, REACH + 1)
    target = jnp.clip(home_dev[:, None] + offset, 0, devices - 1)
    choose = jax.random.randint(key_within, (NBOX, slots), 0, SEL)
    return (home_dev, target, choose)


def draw_near_boxes(key, part):
    picks = box_picks(key)
    key = jax.random.fold_in(key, 11)
    own_box = jnp.arange(NBOX, dtype=jnp.int32)
    home_dev, target, choose = pick_boxes(key, NEAR - 1)
    within = picks[home_dev[:, None], target - home_dev[:, None] + REACH, choose]
    others = target * BOX_DEV + within
    return jnp.concatenate([own_box[:, None], others], axis=1).astype(jnp.int32)


def draw_near_counts(key, part):
    key = jax.random.fold_in(key, 12)
    devices = NBOX // BOX_DEV
    key_base, key_heavy, key_full = jax.random.split(key, 3)
    own_box = jnp.arange(NBOX, dtype=jnp.int32)
    home_dev = own_box // BOX_DEV
    position = own_box % BOX_DEV
    base_count = jax.random.randint(key_base, (NBOX,), 1, NEAR + 1)
    heavy = jax.random.randint(key_heavy, (devices,), 0, 4) == 0
    full_box = jax.random.randint(key_full, (devices,), 0, BOX_DEV)
    filled = heavy[home_dev] | (position == full_box[home_dev])
    return jnp.where(filled, NEAR, base_count).astype(jnp.int32)


def draw_far_boxes(key, part):
    picks = box_picks(key)
    key = jax.random.fold_in(key, 13)
    devices = NBOX // BOX_DEV
    own_box = jnp.arange(NBOX, dtype=jnp.int32)
    position = own_box % BOX_DEV
    home_dev, target, choose = pick_boxes(key, FAR)
    slot_ids = jnp.arange(FAR, dtype=jnp.int32)[None, :]
    forced = (position < SEL)[:, None] & (slot_ids == 0)
    next_dev = jnp.where(home_dev < devices - 1, home_dev + 1, home_dev - 1)
    target = jnp.where(forced, next_dev[:, None], target)
    choose = jnp.where(forced, position[:, None], choose)
    within = picks[home_dev[:, None], target - home_dev[:, None] + REACH, choose]
    return (target * BOX_DEV + within).astype(jnp.int32)


def block_levels(key, shape, shards, smallest, top_value):
    loudness = 1.0
    for axis_at, blocks in shards:
        heights = jax.random.uniform(jax.random.fold_in(jax.random.fold_in(key, 6), axis_at), (blocks,), jnp.float32, smallest / len(shards), top_value / len(shards))
        loudness = loudness * jnp.repeat(jnp.exp(heights), shape[axis_at] // blocks).reshape((-1,) + (1,) * (len(shape) - 1 - axis_at))
    return loudness


def noise(stream_key, shape, spread, most, shards=(), kind=jnp.bfloat16):
    result = spread * jax.random.normal(stream_key, shape, jnp.float32)
    if shards:
        result = result * block_levels(stream_key, shape, shards, -0.22, 0.18)
    return jnp.clip(result, -most, most).astype(kind)


def setup_inputs(seed: int = 0) -> dict:
    splits = jax.random.split(jax.random.key(seed), 12)
    vectors = noise(splits[0], (NBOX, RHS, LEAF), 1.0, 6.0, ((0, 256),))
    leaf_basis = noise(splits[1], (NBOX, RANK, LEAF), LEAF ** -0.5, 0.375, ((0, 256),))
    leaf_transfer = noise(splits[2], (NBOX, RANK, RANK), (RANK * BOX_DEV) ** -0.5, 0.1875, ((0, 256),))
    leaf_coupling = noise(splits[3], (NBOX, RANK, FAR * RANK), (FAR * RANK) ** -0.5, 0.3125, ((0, 256),))
    near_tiles = noise(splits[4], (NBOX, NEAR, LEAF, LEAF), (NEAR * LEAF) ** -0.5, 0.1875, ((0, 256),))
    tile_scale = jnp.clip(jnp.exp(math.log(3.0) - 2.3025851 * jax.random.uniform(splits[5], (NBOX, NEAR), jnp.float32) ** block_levels(splits[5], (NBOX, NEAR), ((0, 256),), -0.2, 0.2)), 0.3, 3.0)
    near_boxes = draw_near_boxes(jax.random.fold_in(splits[11], 71), 0)
    near_counts = draw_near_counts(jax.random.fold_in(splits[11], 71), 0)
    far_boxes = draw_far_boxes(jax.random.fold_in(splits[11], 71), 0)
    level_up = noise(splits[9], (N_PTS, UP, RANK, RANK), RANK ** -0.5, 0.75, ((0, 256),), jnp.float32)
    level_coupling = noise(splits[10], (N_PTS, UP, RANK, RANK), (RANK * UP) ** -0.5, 0.3125, ((0, 256),), jnp.float32)
    return {"vectors": vectors, "leaf_basis": leaf_basis, "leaf_transfer": leaf_transfer, "leaf_coupling": leaf_coupling, "near_tiles": near_tiles, "tile_scale": tile_scale, "near_boxes": near_boxes, "near_counts": near_counts, "far_boxes": far_boxes, "level_up": level_up, "level_coupling": level_coupling}


HIGH = lax.Precision.HIGHEST


def near_field(vectors, tiles, boxes, counts, scales):
    gathered = vectors[boxes].astype(jnp.float32)
    products = jnp.einsum('bsrj,bsij->bsri', gathered, tiles.astype(jnp.float32))
    in_use = (jnp.arange(NEAR, dtype=jnp.int32)[None, :] < counts[:, None]).astype(jnp.float32)
    return jnp.einsum('bsri,bs->bri', products, scales * in_use)


def reference(vectors, leaf_basis, leaf_transfer, leaf_coupling, near_tiles, tile_scale, near_boxes, near_counts, far_boxes, level_up, level_coupling):
    coefficients = jnp.einsum('brj,bij->bri', vectors.astype(jnp.float32), leaf_basis.astype(jnp.float32)).astype(jnp.bfloat16)
    far_coeff = coefficients[far_boxes].astype(jnp.float32)
    coupling = leaf_coupling.astype(jnp.float32).reshape(NBOX, RANK, FAR, RANK)
    leaf_far = jnp.einsum('bsrj,bisj->bri', far_coeff, coupling)
    device_coeff = jnp.einsum('brj,bjk->brk', coefficients.astype(jnp.float32), leaf_transfer.astype(jnp.float32))
    device_coeff = device_coeff.reshape(N_PTS, BOX_DEV, RHS, RANK).sum(axis=1)
    lifted = jnp.einsum('drj,dkjm->dkrm', device_coeff, level_up, precision=HIGH)
    devices = jnp.arange(N_PTS, dtype=jnp.int32)
    far_field = jnp.zeros((N_PTS, RHS, RANK), jnp.float32)
    for bit_level in range(UP):
        grouped = lifted[:, bit_level].reshape(N_PTS // 2 ** bit_level, 2 ** bit_level, RHS, RANK).sum(axis=1)
        sibling = grouped[jnp.bitwise_xor(devices // 2 ** bit_level, 1)]
        far_field = far_field + jnp.einsum('drj,djm->drm', sibling, level_coupling[:, bit_level], precision=HIGH)
    far_rounded = far_field.astype(jnp.bfloat16).astype(jnp.float32)
    transfer_blocks = leaf_transfer.astype(jnp.float32).reshape(N_PTS, BOX_DEV, RANK, RANK)
    pushed = jnp.einsum('drk,dbjk->dbrj', far_rounded, transfer_blocks).reshape(NBOX, RHS, RANK)
    leaf_field = (leaf_far + pushed).astype(jnp.bfloat16)
    far_part = jnp.einsum('bri,bij->brj', leaf_field.astype(jnp.float32), leaf_basis.astype(jnp.float32))

    def one_device(inputs):
        tiles, boxes, counts, scales = inputs
        return near_field(vectors, tiles, boxes, counts, scales)

    near_part = lax.map(one_device, (near_tiles.reshape(N_PTS, BOX_DEV, NEAR, LEAF, LEAF), near_boxes.reshape(N_PTS, BOX_DEV, NEAR), near_counts.reshape(N_PTS, BOX_DEV), tile_scale.reshape(N_PTS, BOX_DEV, NEAR)))
    return far_part + near_part.reshape(NBOX, RHS, LEAF)
```

```python
import jax
import jax.numpy as jnp
from jax import lax
from jax.experimental import pallas as pl
from jax.experimental.pallas import tpu as pltpu
from jax.sharding import PartitionSpec as P

LEAF = 256
RANK = 64
RHS = 8
NEAR = 4
FAR = 6
UP = 5
BOXES = 16
LINE = 8
SEL = 4
SLOTS = 2 * SEL
ROWS = BOXES * RHS
PICKED = SLOTS * RHS
WIDE = LEAF + 2 * RANK
QUAD = 4 * LINE

F32 = jnp.float32
BF16 = jnp.bfloat16
VMEM = pl.BlockSpec(memory_space=pltpu.VMEM)
SMEM = pl.BlockSpec(memory_space=pltpu.SMEM)
ANY = pl.BlockSpec(memory_space=pl.ANY)


def nt(a, b):
    return lax.dot_general(a, b, (((1,), (1,)), ((), ())), preferred_element_type=F32)


def nn(a, b):
    return lax.dot_general(a, b, (((1,), (0,)), ((), ())), preferred_element_type=F32)


def iota(shape, dim):
    return lax.broadcasted_iota(jnp.int32, shape, dim)


def partner_up(line):
    return line ^ 1


def partner_down(line):
    return ((line + 1) ^ 1) - 1


def request_kernel(me_ref, near_ref, far_ref, want_ref, place_ref):
    me = me_ref[0]
    line, home = me >> 3, me & 7

    def parts(shape):
        lane = iota(shape, 1)
        return lane, lane >> 7, (lane >> 4) & 7, lane & 15

    lane, t, p, c = parts((BOXES, 3 * 128))
    lines = jnp.where(t == 0, line, jnp.where(t == 1, partner_up(line), partner_down(line)))
    candidate = ((lines * LINE + p) << 4) + c
    near, far = near_ref[...], far_ref[...]
    columns = [near[:, s : s + 1] for s in range(1, NEAR)] + [far[:, s : s + 1] for s in range(FAR)]
    hits = [column == candidate for column in columns]
    named = hits[0]
    for hit in hits[1:]:
        named = named | hit
    named = jnp.max(named.astype(jnp.int32), axis=0, keepdims=True)

    lane, t, p, c = parts((RHS, 3 * 128))
    own = (t == 0) & (p == home)
    named = jnp.where(own, 0, jnp.broadcast_to(named, (RHS, 3 * 128)))
    ahead = named
    for step in (1, 2, 4, 8):
        ahead = ahead + jnp.where(c >= step, pltpu.roll(ahead, step, 1), 0)
    slot = jnp.where(t == 0, 0, SEL) + jnp.minimum(ahead - named, SEL - 1)

    where = jnp.where(own, LINE * SLOTS + c, p * SLOTS + slot)
    where = jnp.broadcast_to(where[:1], (BOXES, 3 * 128))
    out_lane = iota((BOXES, 128), 1)
    places = jnp.zeros((BOXES, 128), jnp.int32)
    for s, hit in enumerate(hits):
        found = jnp.sum(jnp.where(hit, where, 0), axis=1, keepdims=True)
        places = jnp.where(out_lane == s, found, places)
    place_ref[...] = places

    chosen = (named > 0) & (p == iota((RHS, 3 * 128), 0))
    chosen = jnp.where(chosen, slot + 1, 0).astype(F32).astype(BF16)
    spread = ((iota((128, 128), 0) & 15) == (iota((128, 128), 1) >> 3)).astype(F32).astype(BF16)
    row = iota((RHS, 128), 1) & 7
    for k in range(3):
        value = nn(chosen[:, k * 128 : (k + 1) * 128], spread).astype(jnp.int32)
        want_ref[:, k * 128 : (k + 1) * 128] = jnp.where(value > 0, (value - 1) * RHS + row, -1)


def lift_kernel(vectors_ref, basis_ref, transfer_ref, up_ref, block_ref, top_ref):
    coefficients = []
    total = jnp.zeros((RHS, RANK), F32)
    for b in range(BOXES):
        q = nt(vectors_ref[b], basis_ref[b]).astype(BF16)
        total = total + nn(q, transfer_ref[b])
        coefficients.append(q.astype(F32))
    total = total.astype(BF16)
    lifted = [nn(total, up_ref[0, k].astype(BF16)) for k in range(UP)]
    nothing = jnp.zeros((RHS, RANK), F32)
    lifted_rows = lifted + [nothing] * (BOXES - UP)
    for i in range(BOXES // 2):
        rows = pl.ds(2 * RHS * i, 2 * RHS)
        pair = (2 * i, 2 * i + 1)
        block_ref[rows, :LEAF] = jnp.concatenate(
            [vectors_ref[b].astype(F32) for b in pair], axis=0
        ).astype(BF16)
        block_ref[rows, LEAF:] = jnp.concatenate(
            [jnp.concatenate([coefficients[b], lifted_rows[b]], axis=1) for b in pair], axis=0
        ).astype(BF16)
    top_ref[...] = jnp.concatenate([nothing, lifted[UP - 1]], axis=1)


def pick_kernel(want_ref, own_ref, up_ref, down_ref, top_a_ref, top_b_ref, out_ref):
    data = jnp.concatenate([own_ref[...], up_ref[...], down_ref[...]], axis=0)
    want = want_ref[...]
    picks = jnp.concatenate(
        [
            (jnp.broadcast_to(want[q : q + 1], (PICKED, 3 * 128)) == iota((PICKED, 3 * 128), 0))
            .astype(F32)
            .astype(BF16)
            for q in range(LINE)
        ],
        axis=0,
    )
    own_levels = own_ref[0:32, LEAF:].astype(F32)
    up_levels = up_ref[16:32, LEAF:].astype(F32)
    levels = jnp.concatenate(
        [
            own_levels[:24],
            up_levels[8:16],
            top_a_ref[...] + top_b_ref[...],
            jnp.zeros((PICKED - UP * RHS, 128), F32),
        ],
        axis=0,
    )
    selected = nn(picks, data)
    low = iota((PICKED, 128), 1) < RANK
    for q in range(LINE):
        rows = slice(q * PICKED, (q + 1) * PICKED)
        out_ref[q, :, :LEAF] = selected[rows, :LEAF].astype(BF16)
        out_ref[q, :, LEAF:] = jnp.where(low, selected[rows, LEAF:], levels).astype(BF16)


def final_kernel(
    me_ref,
    place_ref,
    scale_ref,
    count_ref,
    got_any,
    own_any,
    basis_any,
    transfer_any,
    coupling_any,
    level_any,
    tiles_any,
    out_ref,
    got,
    own,
    window,
    basis,
    transfer,
    coupling,
    level,
    tiles,
    sems,
    tile_sems,
):
    pairs = (
        (got_any, got),
        (own_any, own),
        (level_any, level),
        (transfer_any, transfer),
        (coupling_any, coupling),
        (basis_any, basis),
    )
    copies = [pltpu.make_async_copy(a, b, sems.at[i]) for i, (a, b) in enumerate(pairs)]
    tile_copies = [
        pltpu.make_async_copy(tiles_any.at[b], tiles.at[b], tile_sems.at[b]) for b in range(BOXES)
    ]
    for copy in copies + tile_copies:
        copy.start()
    for copy in copies:
        copy.wait()
    home = me_ref[0] & 7
    for p in range(LINE):
        window[p * PICKED : (p + 1) * PICKED, :] = got[p].astype(F32)
    window[LINE * PICKED :, :] = own[...].astype(F32)

    groups = [jnp.zeros((RHS, 128), F32) for _ in range(UP)]
    for p in range(LINE):
        apart = home ^ p
        chunk = window[p * PICKED : p * PICKED + UP * RHS, LEAF:]
        for k in range(UP):
            piece = chunk[k * RHS : (k + 1) * RHS]
            if k < 3:
                piece = jnp.where((apart >> k) == 1, piece, 0.0)
            groups[k] = groups[k] + piece
    far_field = jnp.zeros((RHS, RANK), F32)
    for k in range(UP):
        far_field = far_field + nn(groups[k][:, RANK:].astype(BF16), level[0, k].astype(BF16))
    far_field = far_field.astype(BF16)

    def rows_of(b, s):
        return pl.ds(pl.multiple_of(place_ref[b, s] * RHS, RHS), RHS)

    low = iota((RHS, 128), 1) < RANK
    for b in range(BOXES):
        halves = [window[rows_of(b, NEAR - 1 + s), LEAF:] for s in range(FAR)]
        joined = jnp.concatenate(
            [
                jnp.where(low, halves[2 * i], pltpu.roll(halves[2 * i + 1], RANK, 1))
                for i in range(FAR // 2)
            ],
            axis=1,
        ).astype(BF16)
        leaf = nt(joined, coupling[b]) + nt(far_field, transfer[b])
        total = nn(leaf.astype(BF16), basis[b])
        tile_copies[b].wait()
        for s in range(NEAR):
            if s == 0:
                x = window[(LINE * SLOTS + b) * RHS : (LINE * SLOTS + b + 1) * RHS, :LEAF]
            else:
                x = window[rows_of(b, s - 1), :LEAF]
            weight = jnp.where(s < count_ref[b], scale_ref[b, s], 0.0)
            total = total + weight * nt(x.astype(BF16), tiles[b, s])
        out_ref[b] = total


def pairwise(block, partner):
    count = lax.axis_size("pts")
    route = [(i, partner(i)) for i in range(count) if 0 <= partner(i) < count]
    return lax.ppermute(block, "pts", route)


def per_device(
    vectors,
    leaf_basis,
    leaf_transfer,
    leaf_coupling,
    near_tiles,
    tile_scale,
    near_boxes,
    near_counts,
    far_boxes,
    level_up,
    level_coupling,
):
    count = lax.axis_size("pts")
    lines = [[LINE * i + p for p in range(LINE)] for i in range(count // LINE)]
    me = lax.axis_index("pts").astype(jnp.int32).reshape(1)

    block, top = pl.pallas_call(
        lift_kernel,
        out_shape=(
            jax.ShapeDtypeStruct((ROWS, WIDE), BF16),
            jax.ShapeDtypeStruct((RHS, 128), F32),
        ),
        in_specs=[VMEM] * 4,
        out_specs=(VMEM, VMEM),
        name="lift",
    )(vectors, leaf_basis, leaf_transfer, level_up)

    want, place = pl.pallas_call(
        request_kernel,
        out_shape=(
            jax.ShapeDtypeStruct((LINE, 3 * 128), jnp.int32),
            jax.ShapeDtypeStruct((BOXES, 128), jnp.int32),
        ),
        in_specs=[SMEM, VMEM, VMEM],
        out_specs=(VMEM, VMEM),
        name="request",
    )(me, near_boxes, far_boxes)

    up = pairwise(block, lambda i: LINE * partner_up(i // LINE) + i % LINE)
    down = pairwise(block, lambda i: LINE * partner_down(i // LINE) + i % LINE)
    top_a = pairwise(top, lambda i: i ^ (2 * LINE))
    top_b = pairwise(top, lambda i: i ^ (3 * LINE))
    wanted = lax.all_to_all(
        want.reshape(LINE, 1, 3 * 128), "pts", 0, 0, axis_index_groups=lines
    ).reshape(LINE, 3 * 128)

    parcels = pl.pallas_call(
        pick_kernel,
        out_shape=jax.ShapeDtypeStruct((LINE, PICKED, WIDE), BF16),
        in_specs=[VMEM] * 6,
        out_specs=VMEM,
        name="pick",
    )(wanted, block, up, down, top_a, top_b)
    got = lax.all_to_all(parcels, "pts", 0, 0, axis_index_groups=lines)

    return pl.pallas_call(
        final_kernel,
        out_shape=jax.ShapeDtypeStruct((BOXES, RHS, LEAF), F32),
        in_specs=[SMEM] * 4 + [ANY] * 7,
        out_specs=VMEM,
        scratch_shapes=[
            pltpu.VMEM((LINE, PICKED, WIDE), BF16),
            pltpu.VMEM((ROWS, WIDE), BF16),
            pltpu.VMEM((LINE * PICKED + ROWS, WIDE), F32),
            pltpu.VMEM((BOXES, RANK, LEAF), BF16),
            pltpu.VMEM((BOXES, RANK, RANK), BF16),
            pltpu.VMEM((BOXES, RANK, FAR * RANK), BF16),
            pltpu.VMEM((1, UP, RANK, RANK), F32),
            pltpu.VMEM((BOXES, NEAR, LEAF, LEAF), BF16),
            pltpu.SemaphoreType.DMA((6,)),
            pltpu.SemaphoreType.DMA((BOXES,)),
        ],
        compiler_params=pltpu.CompilerParams(vmem_limit_bytes=24 * 1024 * 1024),
        name="final",
    )(
        me,
        place,
        tile_scale,
        near_counts,
        got,
        block,
        leaf_basis,
        leaf_transfer,
        leaf_coupling,
        level_coupling,
        near_tiles,
    )


def solution(mesh):
    placed = (
        P("pts", None, None),
        P("pts", None, None),
        P("pts", None, None),
        P("pts", None, None),
        P("pts", None, None, None),
        P("pts", None),
        P("pts", None),
        P("pts"),
        P("pts", None),
        P("pts", None, None, None),
        P("pts", None, None, None),
    )
    return jax.shard_map(
        per_device, mesh=mesh, in_specs=placed, out_specs=P("pts", None, None), check_vma=False
    )
```

```python
import jax
import jax.numpy as jnp
from jax import lax
from jax.experimental import pallas as pl
from jax.experimental.pallas import tpu as pltpu
from jax.sharding import PartitionSpec as P

LEAF = 256
RANK = 64
RHS = 8
NEAR = 4
FAR = 6
UP = 5
BOXES = 16
LINE = 8
CHIPS = 4
CORES = 2
WIDE = LEAF + 2 * RANK
MIB = 1024 * 1024

F32 = jnp.float32
BF16 = jnp.bfloat16
I32 = jnp.int32
VMEM = pl.BlockSpec(memory_space=pltpu.VMEM)
SMEM = pl.BlockSpec(memory_space=pltpu.SMEM)
ANY = pl.BlockSpec(memory_space=pl.ANY)


def nt(a, b):
    return lax.dot_general(a, b, (((1,), (1,)), ((), ())), preferred_element_type=F32)


def nn(a, b):
    return lax.dot_general(a, b, (((1,), (0,)), ((), ())), preferred_element_type=F32)


def iota(shape, dim):
    return lax.broadcasted_iota(I32, shape, dim)


def partner_up(line):
    return line ^ 1


def partner_down(line):
    return ((line + 1) ^ 1) - 1


def front_kernel(
    me_ref,
    near_ref,
    far_ref,
    vectors_any,
    basis_any,
    transfer_any,
    up_any,
    block_ref,
    place_ref,
    vectors,
    basis,
    transfer,
    up,
    sems,
):
    pairs = ((vectors_any, vectors), (basis_any, basis), (transfer_any, transfer), (up_any, up))
    copies = [pltpu.make_async_copy(a, b, sems.at[i]) for i, (a, b) in enumerate(pairs)]
    for copy in copies:
        copy.start()
    line, core = me_ref[0] >> 3, me_ref[0] & 1
    for first, ref in ((0, near_ref), (8, far_ref)):
        box = ref[...]
        apart = ((box >> 4) & 1) ^ core
        beside = ((box >> 7) != line).astype(I32)
        place = (apart << 7) | (((box >> 5) & 3) << 5) | (beside << 4) | (box & 15)
        place_ref[first : first + box.shape[0], 0:BOXES] = place
    copies[0].wait()
    copies[1].wait()
    coefficients = [nt(vectors[b], basis[b]).astype(BF16) for b in range(BOXES)]
    copies[2].wait()
    total = jnp.zeros((RHS, RANK), F32)
    for b in range(BOXES):
        total = total + nn(coefficients[b], transfer[b])
    total = total.astype(BF16)
    copies[3].wait()
    lifted = [nn(total, up[0, k].astype(BF16)) for k in range(UP)]
    nothing = jnp.zeros((RHS, RANK), F32)
    for b in range(BOXES):
        block_ref[b, :, :LEAF] = vectors[b]
        extra = lifted[b] if b < UP else nothing
        block_ref[b, :, LEAF:] = jnp.concatenate(
            [coefficients[b].astype(F32), extra], axis=1
        ).astype(BF16)


def pack_kernel(me_ref, own_ref, up_ref, down_ref, top_ref, out_ref):
    me = me_ref[0]
    home, core = me & 7, me & 1
    prev_is_up = ((me >> 3) & 1) == 1
    low = iota((RHS, 128), 1) < RANK
    third = jnp.where(low, own_ref[3, :, LEAF:].astype(F32), up_ref[3, :, LEAF:].astype(F32))
    fourth = jnp.where(low, own_ref[4, :, LEAF:].astype(F32), top_ref[...])
    for chip in range(CHIPS):
        out_ref[chip, 0] = own_ref[...]
        out_ref[chip, 0, 3, :, LEAF:] = third.astype(BF16)
        out_ref[chip, 0, 4, :, LEAF:] = fourth.astype(BF16)
        use_prev = home > 2 * chip + 1 - core
        use_up = use_prev == prev_is_up

        @pl.when(use_up)
        def _():
            out_ref[chip, 1] = up_ref[...]

        @pl.when(jnp.logical_not(use_up))
        def _():
            out_ref[chip, 1] = down_ref[...]


def stage_kernel(
    count_ref,
    scale_ref,
    after_any,
    vectors_any,
    tiles_any,
    basis_any,
    transfer_any,
    coupling_any,
    level_any,
    near_ref,
    basis_ref,
    transfer_ref,
    coupling_ref,
    level_ref,
    kept_ref,
    vectors,
    mine,
    sems,
    keep_sems,
):
    copies = [pltpu.make_async_copy(vectors_any, vectors, keep_sems.at[5])]
    copies += [
        pltpu.make_async_copy(tiles_any.at[pl.ds(b, 4), 0], mine.at[pl.ds(b, 4)], sems.at[b // 4])
        for b in range(0, BOXES, 4)
    ]
    pairs = (
        (tiles_any.at[:, pl.ds(1, NEAR - 1)], kept_ref),
        (coupling_any, coupling_ref),
        (transfer_any, transfer_ref),
        (basis_any, basis_ref),
        (level_any, level_ref),
    )
    keeps = [pltpu.make_async_copy(a, b, keep_sems.at[i]) for i, (a, b) in enumerate(pairs)]
    for copy in copies + keeps:
        copy.start()
    copies[0].wait()
    for first in range(0, BOXES, 4):
        copies[1 + first // 4].wait()
        parts = [nt(vectors[b], mine[b]) for b in range(first, first + 4)]
        for b in range(first, first + 4):
            weight = jnp.where(count_ref[b] > 0, scale_ref[0, b], 0.0)
            near_ref[b] = weight * parts[b - first]
    for keep in keeps:
        keep.wait()


def final_kernel(
    me_ref,
    count_ref,
    scale_ref,
    place_any,
    same_any,
    other_any,
    near,
    basis,
    transfer,
    coupling,
    level,
    tiles,
    out_ref,
    window,
    place,
    sems,
):
    copies = [
        pltpu.make_async_copy(place_any, place, sems.at[0]),
        pltpu.make_async_copy(same_any, window.at[0], sems.at[1]),
        pltpu.make_async_copy(other_any, window.at[1], sems.at[2]),
    ]
    for copy in copies:
        copy.start()
    for copy in copies:
        copy.wait()
    home, core = me_ref[0] & 7, me_ref[0] & 1

    groups = [jnp.zeros((RHS, 128), F32) for _ in range(UP)]
    for half in range(2):
        for chip in range(CHIPS):
            apart = home ^ (2 * chip + (core ^ half))
            for k in range(UP):
                piece = window[half, chip, 0, k, :, LEAF:].astype(F32)
                if k < 3:
                    piece = jnp.where((apart >> k) == 1, piece, 0.0)
                groups[k] = groups[k] + piece
    far_field = jnp.zeros((RHS, RANK), F32)
    for k in range(UP):
        far_field = far_field + nn(groups[k][:, RANK:].astype(BF16), level[0, k].astype(BF16))
    far_field = far_field.astype(BF16)

    def entry(row, b):
        at = place[row, b]
        return at >> 7, (at >> 5) & 3, (at >> 4) & 1, at & 15

    low = iota((RHS, 128), 1) < RANK
    leaves = []
    for b in range(BOXES):
        halves = [window[(*entry(8 + s, b), slice(None), slice(LEAF, WIDE))].astype(F32) for s in range(FAR)]
        joined = jnp.concatenate(
            [
                jnp.where(low, halves[2 * i], pltpu.roll(halves[2 * i + 1], RANK, 1))
                for i in range(FAR // 2)
            ],
            axis=1,
        ).astype(BF16)
        leaves.append(nt(joined, coupling[b]))
    leaves = [(leaves[b] + nt(far_field, transfer[b])).astype(BF16) for b in range(BOXES)]
    for b in range(BOXES):
        out_ref[b] = near[b] + nn(leaves[b], basis[b])
    for first in range(0, BOXES, 2):
        pair = range(first, first + 2)
        parts = [
            [
                nt(window[(*entry(s, b), slice(None), slice(0, LEAF))], tiles[b, s - 1])
                for s in range(1, NEAR)
            ]
            for b in pair
        ]
        for b in pair:
            total = out_ref[b]
            for s in range(1, NEAR):
                weight = jnp.where(s < count_ref[b], scale_ref[s, b], 0.0)
                total = total + weight * parts[b - first][s - 1]
            out_ref[b] = total


def pairwise(block, partner):
    count = lax.axis_size("pts")
    route = [(i, partner(i)) for i in range(count) if 0 <= partner(i) < count]
    return lax.ppermute(block, "pts", route)


def shape_of(shape, dtype):
    return jax.ShapeDtypeStruct(shape, dtype)


def per_device(
    vectors,
    leaf_basis,
    leaf_transfer,
    leaf_coupling,
    near_tiles,
    tile_scale,
    near_boxes,
    near_counts,
    far_boxes,
    level_up,
    level_coupling,
):
    count = lax.axis_size("pts")
    rows = [
        [LINE * i + CORES * c + k for c in range(CHIPS)]
        for i in range(count // LINE)
        for k in range(CORES)
    ]
    me = lax.axis_index("pts").astype(I32).reshape(1)
    scales = tile_scale.T

    def off(x):
        return pltpu.with_memory_space_constraint(x, pltpu.HBM)

    block, place = pl.pallas_call(
        front_kernel,
        out_shape=(
            shape_of((BOXES, RHS, WIDE), BF16),
            shape_of((BOXES, 128), I32),
        ),
        in_specs=[SMEM, VMEM, VMEM] + [ANY] * 4,
        out_specs=(VMEM,) * 2,
        scratch_shapes=[
            pltpu.VMEM((BOXES, RHS, LEAF), BF16),
            pltpu.VMEM((BOXES, RANK, LEAF), BF16),
            pltpu.VMEM((BOXES, RANK, RANK), BF16),
            pltpu.VMEM((1, UP, RANK, RANK), F32),
            pltpu.SemaphoreType.DMA((4,)),
        ],
        compiler_params=pltpu.CompilerParams(vmem_limit_bytes=8 * MIB),
        name="front",
    )(
        me,
        off(near_boxes.T),
        off(far_boxes.T),
        off(vectors),
        off(leaf_basis),
        off(leaf_transfer),
        off(level_up),
    )

    up = pairwise(block, lambda i: LINE * partner_up(i // LINE) + i % LINE)
    down = pairwise(block, lambda i: LINE * partner_down(i // LINE) + i % LINE)
    tops = block[UP - 1, :, LEAF:].astype(F32) + up[UP - 1, :, LEAF:].astype(F32)
    top = pairwise(tops, lambda i: i ^ (2 * LINE))

    parcels = pl.pallas_call(
        pack_kernel,
        out_shape=shape_of((CHIPS, 2, BOXES, RHS, WIDE), BF16),
        in_specs=[SMEM] + [VMEM] * 4,
        out_specs=VMEM,
        compiler_params=pltpu.CompilerParams(vmem_limit_bytes=8 * MIB),
        name="pack",
    )(me, block, up, down, top)
    same = lax.all_to_all(parcels, "pts", 0, 0, axis_index_groups=rows)
    other = pairwise(same, lambda i: i ^ 1)

    near, basis, transfer, coupling, level, kept = pl.pallas_call(
        stage_kernel,
        out_shape=(
            pltpu.VMEM((BOXES, RHS, LEAF), F32),
            pltpu.VMEM((BOXES, RANK, LEAF), BF16),
            pltpu.VMEM((BOXES, RANK, RANK), BF16),
            pltpu.VMEM((BOXES, RANK, FAR * RANK), BF16),
            pltpu.VMEM((1, UP, RANK, RANK), F32),
            pltpu.VMEM((BOXES, NEAR - 1, LEAF, LEAF), BF16),
        ),
        in_specs=[SMEM, SMEM] + [ANY] * 7,
        out_specs=(VMEM,) + (ANY,) * 5,
        scratch_shapes=[
            pltpu.VMEM((BOXES, RHS, LEAF), BF16),
            pltpu.VMEM((BOXES, LEAF, LEAF), BF16),
            pltpu.SemaphoreType.DMA((4,)),
            pltpu.SemaphoreType.DMA((6,)),
        ],
        compiler_params=pltpu.CompilerParams(vmem_limit_bytes=16 * MIB),
        name="stage",
    )(
        off(near_counts),
        off(scales),
        parcels,
        off(vectors),
        off(near_tiles),
        off(leaf_basis),
        off(leaf_transfer),
        off(leaf_coupling),
        off(level_coupling),
    )

    return pl.pallas_call(
        final_kernel,
        out_shape=shape_of((BOXES, RHS, LEAF), F32),
        in_specs=[SMEM] * 3 + [ANY] * 3 + [VMEM] * 6,
        out_specs=VMEM,
        scratch_shapes=[
            pltpu.VMEM((2, CHIPS, 2, BOXES, RHS, WIDE), BF16),
            pltpu.SMEM((BOXES, 128), I32),
            pltpu.SemaphoreType.DMA((3,)),
        ],
        compiler_params=pltpu.CompilerParams(vmem_limit_bytes=16 * MIB),
        name="final",
    )(
        me,
        off(near_counts),
        off(scales),
        place,
        same,
        other,
        near,
        basis,
        transfer,
        coupling,
        level,
        kept,
    )


def solution(mesh):
    placed = (
        P("pts", None, None),
        P("pts", None, None),
        P("pts", None, None),
        P("pts", None, None),
        P("pts", None, None, None),
        P("pts", None),
        P("pts", None),
        P("pts"),
        P("pts", None),
        P("pts", None, None, None),
        P("pts", None, None, None),
    )
    return jax.shard_map(
        per_device, mesh=mesh, in_specs=placed, out_specs=P("pts", None, None), check_vma=False
    )
```

```python
import jax
import jax.numpy as jnp
from jax import lax
from jax.experimental import pallas as pl
from jax.experimental.pallas import tpu as pltpu
from jax.sharding import PartitionSpec as P

LEAF = 256
RANK = 64
RHS = 8
NEAR = 4
FAR = 6
UP = 5
BOXES = 16
LINE = 8
CHIPS = 4
CORES = 2
WIDE = LEAF + 2 * RANK
MIB = 1024 * 1024

F32 = jnp.float32
BF16 = jnp.bfloat16
I32 = jnp.int32
VMEM = pl.BlockSpec(memory_space=pltpu.VMEM)
SMEM = pl.BlockSpec(memory_space=pltpu.SMEM)
ANY = pl.BlockSpec(memory_space=pl.ANY)


def nt(a, b):
    return lax.dot_general(a, b, (((1,), (1,)), ((), ())), preferred_element_type=F32)


def nn(a, b):
    return lax.dot_general(a, b, (((1,), (0,)), ((), ())), preferred_element_type=F32)


def iota(shape, dim):
    return lax.broadcasted_iota(I32, shape, dim)


def partner_up(line):
    return line ^ 1


def partner_down(line):
    return ((line + 1) ^ 1) - 1


def front_kernel(
    me_ref,
    near_any,
    far_any,
    count_any,
    scale_any,
    vectors_any,
    basis_any,
    transfer_any,
    up_any,
    block_ref,
    place_ref,
    weight_ref,
    near,
    far,
    count,
    scale,
    vectors,
    basis,
    transfer,
    up,
    sems,
):
    pairs = (
        (vectors_any, vectors),
        (basis_any, basis),
        (transfer_any, transfer),
        (up_any, up),
        (near_any, near),
        (far_any, far),
        (count_any, count),
        (scale_any, scale),
    )
    copies = [pltpu.make_async_copy(a, b, sems.at[i]) for i, (a, b) in enumerate(pairs)]
    for copy in copies:
        copy.start()
    copies[0].wait()
    copies[1].wait()
    coefficients = [nt(vectors[b], basis[b]).astype(BF16) for b in range(BOXES)]
    copies[2].wait()
    total = jnp.zeros((RHS, RANK), F32)
    for b in range(BOXES):
        total = total + nn(coefficients[b], transfer[b])
    total = total.astype(BF16)
    copies[3].wait()
    lifted = [nn(total, up[0, k].astype(BF16)) for k in range(UP)]
    nothing = jnp.zeros((RHS, RANK), F32)
    for b in range(BOXES):
        block_ref[b, :, :LEAF] = vectors[b]
        extra = lifted[b] if b < UP else nothing
        block_ref[b, :, LEAF:] = jnp.concatenate(
            [coefficients[b].astype(F32), extra], axis=1
        ).astype(BF16)
    for copy in copies[4:]:
        copy.wait()
    me = me_ref[0]
    line, home, core = me >> 3, (me >> 1) & 3, me & 1
    place_ref[...] = jnp.full((BOXES, 128), me, I32)
    for first, ref in ((0, near), (8, far)):
        box = ref[...]
        apart = ((box >> 4) & 1) ^ core
        beside = ((box >> 7) != line).astype(I32)
        chip = ((box >> 5) & 3) ^ home
        place = (apart << 7) | (beside << 6) | (chip << 4) | (box & 15)
        place_ref[first : first + box.shape[0], 0:BOXES] = place
    used = iota((NEAR, BOXES), 0) < jnp.broadcast_to(count[...].reshape(1, BOXES), (NEAR, BOXES))
    weight_ref[0:NEAR, 0:BOXES] = jnp.where(used, scale[...], 0.0)


def join_kernel(near_any, own_ref, first_ref, second_ref, third_ref, line_ref, top_ref):
    top = jnp.zeros((RHS, 128), F32)
    for k, ref in enumerate((own_ref, first_ref, second_ref, third_ref)):
        line_ref[k] = ref[...]
        top = top + ref[UP - 1, :, LEAF:].astype(F32)
    top_ref[...] = top


def pack_kernel(me_ref, ready_any, line_ref, up_ref, down_ref, third, top_a, top_b, out_ref):
    me = me_ref[0]
    home, core = me & 7, me & 1
    prev_is_up = ((me >> 3) & 1) == 1
    out_ref[0] = line_ref[...]
    for k in range(CHIPS):
        use_prev = (home ^ (2 * k)) > home if k else core == 1
        use_up = use_prev == prev_is_up

        @pl.when(use_up)
        def _():
            out_ref[1, k] = up_ref[k]

        @pl.when(jnp.logical_not(use_up))
        def _():
            out_ref[1, k] = down_ref[k]

    low = iota((RHS, 128), 1) < RANK
    for box, levels in ((3, third[...]), (4, top_a[...] + top_b[...])):
        mixed = jnp.where(low, line_ref[0, box, :, LEAF:].astype(F32), levels)
        out_ref[0, 0, box, :, LEAF:] = mixed.astype(BF16)


def own_kernel(weight_any, after_any, vectors_any, tiles_any, near_ref, weight, vectors, mine, sems):
    copies = [
        pltpu.make_async_copy(vectors_any, vectors, sems.at[4]),
        pltpu.make_async_copy(weight_any, weight, sems.at[5]),
    ]
    parts = [
        pltpu.make_async_copy(tiles_any.at[pl.ds(b, 4), 0], mine.at[pl.ds(b, 4)], sems.at[b // 4])
        for b in range(0, BOXES, 4)
    ]
    for copy in copies + parts:
        copy.start()
    for copy in copies:
        copy.wait()
    for first in range(0, BOXES, 4):
        parts[first // 4].wait()
        products = [nt(vectors[b], mine[b]) for b in range(first, first + 4)]
        for b in range(first, first + 4):
            near_ref[b] = weight[0, b] * products[b - first]


def stage_kernel(
    after_any,
    tiles_any,
    basis_any,
    transfer_any,
    coupling_any,
    level_any,
    tiles_ref,
    basis_ref,
    transfer_ref,
    coupling_ref,
    level_ref,
    ready_ref,
    sems,
):
    pairs = (
        (tiles_any.at[:, pl.ds(1, NEAR - 1)], tiles_ref),
        (coupling_any, coupling_ref),
        (transfer_any, transfer_ref),
        (basis_any, basis_ref),
        (level_any, level_ref),
    )
    copies = [pltpu.make_async_copy(a, b, sems.at[i]) for i, (a, b) in enumerate(pairs)]
    for copy in copies:
        copy.start()
    ready_ref[...] = jnp.zeros((8, 128), F32)
    for copy in copies:
        copy.wait()


def final_kernel(
    place_any,
    weight_any,
    same_any,
    other_any,
    near,
    tiles,
    basis,
    transfer,
    coupling,
    level,
    out_any,
    window,
    place,
    weight,
    out,
    sems,
    out_sems,
):
    pairs = (
        (place_any, place),
        (weight_any, weight),
        (same_any, window.at[0]),
        (other_any, window.at[1]),
    )
    copies = [pltpu.make_async_copy(a, b, sems.at[i]) for i, (a, b) in enumerate(pairs)]
    for copy in copies:
        copy.start()
    for copy in copies:
        copy.wait()

    def entry(row, b):
        at = place[row, b]
        return at >> 7, (at >> 6) & 1, (at >> 4) & 3, at & 15

    def levels(half, k, level):
        return window[half, 0, k, level, :, LEAF:].astype(F32)

    groups = [
        levels(1, 0, 0),
        levels(0, 1, 1) + levels(1, 1, 1),
        levels(0, 2, 2) + levels(1, 2, 2) + levels(0, 3, 2) + levels(1, 3, 2),
        levels(0, 0, 3) + levels(1, 0, 3),
        levels(0, 0, 4) + levels(1, 0, 4),
    ]
    far_field = jnp.zeros((RHS, RANK), F32)
    for k in range(UP):
        far_field = far_field + nn(groups[k][:, RANK:].astype(BF16), level[0, k].astype(BF16))
    far_field = far_field.astype(BF16)

    low = iota((RHS, 128), 1) < RANK
    leaves = []
    for b in range(BOXES):
        halves = [
            window[(*entry(8 + s, b), slice(None), slice(LEAF, WIDE))].astype(F32)
            for s in range(FAR)
        ]
        joined = jnp.concatenate(
            [
                jnp.where(low, halves[2 * i], pltpu.roll(halves[2 * i + 1], RANK, 1))
                for i in range(FAR // 2)
            ],
            axis=1,
        ).astype(BF16)
        leaves.append(nt(joined, coupling[b]))
    leaves = [(leaves[b] + nt(far_field, transfer[b])).astype(BF16) for b in range(BOXES)]
    for b in range(BOXES):
        out[b] = near[b] + nn(leaves[b], basis[b])
    outs = []
    for first in range(0, BOXES, 2):
        parts = [
            [
                nt(window[(*entry(s, b), slice(None), slice(0, LEAF))], tiles[b, s - 1])
                for s in range(1, NEAR)
            ]
            for b in range(first, first + 2)
        ]
        for b in range(first, first + 2):
            total = out[b]
            for s in range(1, NEAR):
                total = total + weight[s, b] * parts[b - first][s - 1]
            out[b] = total
        if first % 8 == 6:
            rows = pl.ds(first - 6, 8)
            outs.append(
                pltpu.make_async_copy(out.at[rows], out_any.at[rows], out_sems.at[first // 8])
            )
            outs[-1].start()
    for copy in outs:
        copy.wait()


def pairwise(block, partner):
    count = lax.axis_size("pts")
    route = [(i, partner(i)) for i in range(count) if 0 <= partner(i) < count]
    return lax.ppermute(block, "pts", route)


def shape_of(shape, dtype):
    return jax.ShapeDtypeStruct(shape, dtype)


def per_device(
    vectors,
    leaf_basis,
    leaf_transfer,
    leaf_coupling,
    near_tiles,
    tile_scale,
    near_boxes,
    near_counts,
    far_boxes,
    level_up,
    level_coupling,
):
    me = lax.axis_index("pts").astype(I32).reshape(1)

    def off(x):
        return pltpu.with_memory_space_constraint(x, pltpu.HBM)

    block, place, weight = pl.pallas_call(
        front_kernel,
        out_shape=(
            shape_of((BOXES, RHS, WIDE), BF16),
            shape_of((BOXES, 128), I32),
            shape_of((8, 128), F32),
        ),
        in_specs=[SMEM] + [ANY] * 8,
        out_specs=(VMEM,) * 3,
        scratch_shapes=[
            pltpu.VMEM((NEAR, BOXES), I32),
            pltpu.VMEM((FAR, BOXES), I32),
            pltpu.VMEM((BOXES,), I32),
            pltpu.VMEM((NEAR, BOXES), F32),
            pltpu.VMEM((BOXES, RHS, LEAF), BF16),
            pltpu.VMEM((BOXES, RANK, LEAF), BF16),
            pltpu.VMEM((BOXES, RANK, RANK), BF16),
            pltpu.VMEM((1, UP, RANK, RANK), F32),
            pltpu.SemaphoreType.DMA((8,)),
        ],
        compiler_params=pltpu.CompilerParams(vmem_limit_bytes=8 * MIB),
        name="front",
    )(
        me,
        off(near_boxes.T),
        off(far_boxes.T),
        off(near_counts),
        off(tile_scale.T),
        off(vectors),
        off(leaf_basis),
        off(leaf_transfer),
        off(level_up),
    )

    near = pl.pallas_call(
        own_kernel,
        out_shape=shape_of((BOXES, RHS, LEAF), F32),
        in_specs=[ANY] * 4,
        out_specs=VMEM,
        scratch_shapes=[
            pltpu.SMEM((8, 128), F32),
            pltpu.VMEM((BOXES, RHS, LEAF), BF16),
            pltpu.VMEM((BOXES, LEAF, LEAF), BF16),
            pltpu.SemaphoreType.DMA((6,)),
        ],
        compiler_params=pltpu.CompilerParams(vmem_limit_bytes=8 * MIB),
        name="own",
    )(weight, block, off(vectors), off(near_tiles))

    line, tops = pl.pallas_call(
        join_kernel,
        out_shape=(
            shape_of((CHIPS, BOXES, RHS, WIDE), BF16),
            shape_of((RHS, 128), F32),
        ),
        in_specs=[ANY] + [VMEM] * CHIPS,
        out_specs=(VMEM, VMEM),
        compiler_params=pltpu.CompilerParams(vmem_limit_bytes=4 * MIB),
        name="join",
    )(
        near,
        block,
        *[pairwise(block, lambda i, k=k: i ^ (CORES * k)) for k in range(1, CHIPS)],
    )

    tiles, basis, transfer, coupling, level, ready = pl.pallas_call(
        stage_kernel,
        out_shape=(
            pltpu.VMEM((BOXES, NEAR - 1, LEAF, LEAF), BF16),
            pltpu.VMEM((BOXES, RANK, LEAF), BF16),
            pltpu.VMEM((BOXES, RANK, RANK), BF16),
            pltpu.VMEM((BOXES, RANK, FAR * RANK), BF16),
            pltpu.VMEM((1, UP, RANK, RANK), F32),
            shape_of((8, 128), F32),
        ),
        in_specs=[ANY] * 6,
        out_specs=(ANY,) * 5 + (VMEM,),
        scratch_shapes=[pltpu.SemaphoreType.DMA((5,))],
        compiler_params=pltpu.CompilerParams(vmem_limit_bytes=4 * MIB),
        name="stage",
    )(
        tops,
        off(near_tiles),
        off(leaf_basis),
        off(leaf_transfer),
        off(leaf_coupling),
        off(level_coupling),
    )

    up = pairwise(line, lambda i: LINE * partner_up(i // LINE) + i % LINE)
    down = pairwise(line, lambda i: LINE * partner_down(i // LINE) + i % LINE)
    third = up[:, 3, :, LEAF:].astype(F32).sum(axis=0)
    top_a = pairwise(tops, lambda i: i ^ (2 * LINE))
    top_b = pairwise(tops, lambda i: i ^ (3 * LINE))
    same = pl.pallas_call(
        pack_kernel,
        out_shape=shape_of((2, CHIPS, BOXES, RHS, WIDE), BF16),
        in_specs=[SMEM, ANY] + [VMEM] * 6,
        out_specs=VMEM,
        compiler_params=pltpu.CompilerParams(vmem_limit_bytes=4 * MIB),
        name="pack",
    )(me, ready, line, up, down, third, top_a, top_b)
    other = pairwise(same, lambda i: i ^ 1)

    return pl.pallas_call(
        final_kernel,
        out_shape=shape_of((BOXES, RHS, LEAF), F32),
        in_specs=[ANY] * 4 + [VMEM] * 6,
        out_specs=ANY,
        scratch_shapes=[
            pltpu.VMEM((CORES, 2, CHIPS, BOXES, RHS, WIDE), BF16),
            pltpu.SMEM((BOXES, 128), I32),
            pltpu.SMEM((8, 128), F32),
            pltpu.VMEM((BOXES, RHS, LEAF), F32),
            pltpu.SemaphoreType.DMA((4,)),
            pltpu.SemaphoreType.DMA((2,)),
        ],
        compiler_params=pltpu.CompilerParams(vmem_limit_bytes=16 * MIB),
        name="final",
    )(place, weight, same, other, near, tiles, basis, transfer, coupling, level)


def solution(mesh):
    placed = (
        P("pts", None, None),
        P("pts", None, None),
        P("pts", None, None),
        P("pts", None, None),
        P("pts", None, None, None),
        P("pts", None),
        P("pts", None),
        P("pts"),
        P("pts", None),
        P("pts", None, None, None),
        P("pts", None, None, None),
    )
    return jax.shard_map(
        per_device, mesh=mesh, in_specs=placed, out_specs=P("pts", None, None), check_vma=False
    )
```

```python
import jax
import jax.numpy as jnp
from jax import lax
from jax.experimental import pallas as pl
from jax.experimental.pallas import tpu as pltpu
from jax.sharding import PartitionSpec as P

LEAF = 256
RANK = 64
RHS = 8
NEAR = 4
FAR = 6
UP = 5
BOXES = 16
LINE = 8
CHIPS = 4
CORES = 2
PER_ROW = LEAF // RANK
Q_ROW = BOXES
LIFT_ROW = Q_ROW + BOXES // PER_ROW
ROWS = LIFT_ROW + 2
MIB = 1024 * 1024

F32 = jnp.float32
BF16 = jnp.bfloat16
I32 = jnp.int32
VMEM = pl.BlockSpec(memory_space=pltpu.VMEM)
SMEM = pl.BlockSpec(memory_space=pltpu.SMEM)
ANY = pl.BlockSpec(memory_space=pl.ANY)


def nt(a, b):
    return lax.dot_general(a, b, (((1,), (1,)), ((), ())), preferred_element_type=F32)


def nn(a, b):
    return lax.dot_general(a, b, (((1,), (0,)), ((), ())), preferred_element_type=F32)


def iota(shape, dim):
    return lax.broadcasted_iota(I32, shape, dim)


def partner_up(line):
    return line ^ 1


def partner_down(line):
    return ((line + 1) ^ 1) - 1


def front_kernel(
    me_ref,
    near_any,
    far_any,
    count_any,
    scale_any,
    vectors_any,
    basis_any,
    transfer_any,
    up_any,
    block_ref,
    place_ref,
    weight_ref,
    near,
    far,
    count,
    scale,
    vectors,
    basis,
    transfer,
    up,
    sems,
):
    pairs = (
        (vectors_any, vectors),
        (basis_any, basis),
        (transfer_any, transfer),
        (up_any, up),
        (near_any, near),
        (far_any, far),
        (count_any, count),
        (scale_any, scale),
    )
    copies = [pltpu.make_async_copy(a, b, sems.at[i]) for i, (a, b) in enumerate(pairs)]
    for copy in copies[4:] + copies[:4]:
        copy.start()
    for copy in copies[4:]:
        copy.wait()
    me = me_ref[0]
    line, home, core = me >> 3, (me >> 1) & 3, me & 1
    place_ref[...] = jnp.full((BOXES, 128), me, I32)
    for first, ref in ((0, near), (8, far)):
        box = ref[...]
        apart = ((box >> 4) & 1) ^ core
        beside = ((box >> 7) != line).astype(I32)
        chip = ((box >> 5) & 3) ^ home
        place = (apart << 7) | (beside << 6) | (chip << 4) | (box & 15)
        place_ref[first : first + box.shape[0], 0:BOXES] = place
    used = iota((NEAR, BOXES), 0) < jnp.broadcast_to(count[...].reshape(1, BOXES), (NEAR, BOXES))
    weight_ref[0:NEAR, 0:BOXES] = jnp.where(used, scale[...], 0.0)
    copies[0].wait()
    copies[1].wait()
    coefficients = [nt(vectors[b], basis[b]).astype(BF16) for b in range(BOXES)]
    copies[2].wait()
    total = jnp.zeros((RHS, RANK), F32)
    for b in range(BOXES):
        total = total + nn(coefficients[b], transfer[b])
    total = total.astype(BF16)
    copies[3].wait()
    lifted = [nn(total, up[0, k].astype(BF16)) for k in range(UP)]
    nothing = jnp.zeros((RHS, RANK), F32)
    block_ref[:BOXES] = vectors[...]

    def put(row, pieces):
        block_ref[row] = jnp.concatenate(pieces, axis=1).astype(BF16)

    for j in range(PER_ROW):
        put(Q_ROW + j, [coefficients[PER_ROW * g + j].astype(F32) for g in range(PER_ROW)])
    put(LIFT_ROW, lifted[:4])
    put(LIFT_ROW + 1, [lifted[4], nothing, nothing, nothing])


def join_kernel(ready_any, own_ref, first_ref, second_ref, third_ref, line_ref, top_ref):
    top = jnp.zeros((RHS, 128), F32)
    for k, ref in enumerate((own_ref, first_ref, second_ref, third_ref)):
        line_ref[k] = ref[...]
        top = top + ref[LIFT_ROW + 1, :, :128].astype(F32)
    top_ref[...] = top


def pack_kernel(me_ref, line_ref, up_ref, down_ref, third, top, out_ref):
    me = me_ref[0]
    home, core = me & 7, me & 1
    prev_is_up = ((me >> 3) & 1) == 1
    out_ref[0] = line_ref[...]
    for k in range(CHIPS):
        use_prev = (home ^ (2 * k)) > home if k else core == 1
        use_up = use_prev == prev_is_up

        @pl.when(use_up)
        def _():
            out_ref[1, k] = up_ref[k]

        @pl.when(jnp.logical_not(use_up))
        def _():
            out_ref[1, k] = down_ref[k]

    low = iota((RHS, 128), 1) < RANK
    mixed = jnp.where(low, line_ref[0, LIFT_ROW, :, 128:].astype(F32), third[...])
    out_ref[0, 0, LIFT_ROW, :, 128:] = mixed.astype(BF16)
    out_ref[0, 0, LIFT_ROW + 1, :, :128] = top[...].astype(BF16)


def own_kernel(weight_any, after_any, vectors_any, tiles_any, near_ref, weight, vectors, mine, sems):
    copies = [
        pltpu.make_async_copy(vectors_any, vectors, sems.at[4]),
        pltpu.make_async_copy(weight_any, weight, sems.at[5]),
    ]
    parts = [
        pltpu.make_async_copy(tiles_any.at[pl.ds(b, 4), 0], mine.at[pl.ds(b, 4)], sems.at[b // 4])
        for b in range(0, BOXES, 4)
    ]
    for copy in copies + parts:
        copy.start()
    for copy in copies:
        copy.wait()
    for first in range(0, BOXES, 4):
        parts[first // 4].wait()
        products = [nt(vectors[b], mine[b]) for b in range(first, first + 4)]
        for b in range(first, first + 4):
            near_ref[b] = weight[0, b] * products[b - first]


def stage_kernel(
    after_any,
    tiles_any,
    basis_any,
    transfer_any,
    coupling_any,
    level_any,
    tiles_ref,
    basis_ref,
    transfer_ref,
    coupling_ref,
    level_ref,
    ready_ref,
    sems,
):
    pairs = (
        (tiles_any.at[:, pl.ds(1, NEAR - 1)], tiles_ref),
        (coupling_any, coupling_ref),
        (transfer_any, transfer_ref),
        (basis_any, basis_ref),
        (level_any, level_ref),
    )
    copies = [pltpu.make_async_copy(a, b, sems.at[i]) for i, (a, b) in enumerate(pairs)]
    for copy in copies:
        copy.start()
    ready_ref[...] = jnp.zeros((8, 128), F32)
    for copy in copies:
        copy.wait()


def final_kernel(
    place_any,
    weight_any,
    same_any,
    other_any,
    near,
    tiles,
    basis,
    transfer,
    coupling,
    level,
    out_any,
    window,
    place,
    weight,
    out,
    sems,
    out_sems,
):
    pairs = (
        (place_any, place),
        (weight_any, weight),
        (same_any, window.at[0]),
        (other_any, window.at[1]),
    )
    copies = [pltpu.make_async_copy(a, b, sems.at[i]) for i, (a, b) in enumerate(pairs)]
    for copy in copies:
        copy.start()
    for copy in copies:
        copy.wait()

    def entry(row, b):
        at = place[row, b]
        return at >> 7, (at >> 6) & 1, (at >> 4) & 3, at & 15

    def levels(half, k, level):
        row, lane = LIFT_ROW + level // PER_ROW, level % PER_ROW * RANK
        return window[half, 0, k, row].astype(F32)[:, lane : lane + RANK]

    for first in range(0, BOXES, 2):
        parts = [
            [nt(window[entry(s, b)], tiles[b, s - 1]) for s in range(1, NEAR)]
            for b in range(first, first + 2)
        ]
        for b in range(first, first + 2):
            total = near[b]
            for s in range(1, NEAR):
                total = total + weight[s, b] * parts[b - first][s - 1]
            out[b] = total

    groups = [
        levels(1, 0, 0),
        levels(0, 1, 1) + levels(1, 1, 1),
        levels(0, 2, 2) + levels(1, 2, 2) + levels(0, 3, 2) + levels(1, 3, 2),
        levels(0, 0, 3) + levels(1, 0, 3),
        levels(0, 0, 4) + levels(1, 0, 4),
    ]
    far_field = jnp.zeros((RHS, RANK), F32)
    for k in range(UP):
        far_field = far_field + nn(groups[k].astype(BF16), level[0, k].astype(BF16))
    far_field = far_field.astype(BF16)

    low = iota((RHS, 128), 1) < RANK

    def coefficient(row, b, odd):
        half, line, k, box = entry(row, b)
        lanes = pl.ds(pl.multiple_of((box >> 3) * 128, 128), 128)
        piece = window[half, line, k, Q_ROW + (box & 3), :, lanes].astype(F32)
        return pltpu.roll(piece, (((box >> 2) & 1) ^ odd) * RANK, 1)

    leaves = []
    for b in range(BOXES):
        halves = [coefficient(8 + s, b, s & 1) for s in range(FAR)]
        joined = jnp.concatenate(
            [jnp.where(low, halves[2 * i], halves[2 * i + 1]) for i in range(FAR // 2)], axis=1
        ).astype(BF16)
        leaves.append(nt(joined, coupling[b]))
    leaves = [(leaves[b] + nt(far_field, transfer[b])).astype(BF16) for b in range(BOXES)]
    outs = []
    for b in range(BOXES):
        out[b] = out[b] + nn(leaves[b], basis[b])
        if b % 8 == 7:
            rows = pl.ds(b - 7, 8)
            outs.append(
                pltpu.make_async_copy(out.at[rows], out_any.at[rows], out_sems.at[b // 8])
            )
            outs[-1].start()
    for copy in outs:
        copy.wait()


def pairwise(block, partner):
    count = lax.axis_size("pts")
    route = [(i, partner(i)) for i in range(count) if 0 <= partner(i) < count]
    return lax.ppermute(block, "pts", route)


def shape_of(shape, dtype):
    return jax.ShapeDtypeStruct(shape, dtype)


def per_device(
    vectors,
    leaf_basis,
    leaf_transfer,
    leaf_coupling,
    near_tiles,
    tile_scale,
    near_boxes,
    near_counts,
    far_boxes,
    level_up,
    level_coupling,
):
    me = lax.axis_index("pts").astype(I32).reshape(1)

    def off(x):
        return pltpu.with_memory_space_constraint(x, pltpu.HBM)

    block, place, weight = pl.pallas_call(
        front_kernel,
        out_shape=(
            shape_of((ROWS, RHS, LEAF), BF16),
            shape_of((BOXES, 128), I32),
            shape_of((8, 128), F32),
        ),
        in_specs=[SMEM] + [ANY] * 8,
        out_specs=(VMEM,) * 3,
        scratch_shapes=[
            pltpu.VMEM((NEAR, BOXES), I32),
            pltpu.VMEM((FAR, BOXES), I32),
            pltpu.VMEM((BOXES,), I32),
            pltpu.VMEM((NEAR, BOXES), F32),
            pltpu.VMEM((BOXES, RHS, LEAF), BF16),
            pltpu.VMEM((BOXES, RANK, LEAF), BF16),
            pltpu.VMEM((BOXES, RANK, RANK), BF16),
            pltpu.VMEM((1, UP, RANK, RANK), F32),
            pltpu.SemaphoreType.DMA((8,)),
        ],
        compiler_params=pltpu.CompilerParams(vmem_limit_bytes=8 * MIB),
        name="front",
    )(
        me,
        off(near_boxes.T),
        off(far_boxes.T),
        off(near_counts),
        off(tile_scale.T),
        off(vectors),
        off(leaf_basis),
        off(leaf_transfer),
        off(level_up),
    )

    tiles, basis, transfer, coupling, level, ready = pl.pallas_call(
        stage_kernel,
        out_shape=(
            pltpu.VMEM((BOXES, NEAR - 1, LEAF, LEAF), BF16),
            pltpu.VMEM((BOXES, RANK, LEAF), BF16),
            pltpu.VMEM((BOXES, RANK, RANK), BF16),
            pltpu.VMEM((BOXES, RANK, FAR * RANK), BF16),
            pltpu.VMEM((1, UP, RANK, RANK), F32),
            shape_of((8, 128), F32),
        ),
        in_specs=[ANY] * 6,
        out_specs=(ANY,) * 5 + (VMEM,),
        scratch_shapes=[pltpu.SemaphoreType.DMA((5,))],
        compiler_params=pltpu.CompilerParams(vmem_limit_bytes=4 * MIB),
        name="stage",
    )(
        block,
        off(near_tiles),
        off(leaf_basis),
        off(leaf_transfer),
        off(leaf_coupling),
        off(level_coupling),
    )

    line, tops = pl.pallas_call(
        join_kernel,
        out_shape=(
            shape_of((CHIPS, ROWS, RHS, LEAF), BF16),
            shape_of((RHS, 128), F32),
        ),
        in_specs=[ANY] + [VMEM] * CHIPS,
        out_specs=(VMEM, VMEM),
        compiler_params=pltpu.CompilerParams(vmem_limit_bytes=4 * MIB),
        name="join",
    )(
        ready,
        block,
        *[pairwise(block, lambda i, k=k: i ^ (CORES * k)) for k in range(1, CHIPS)],
    )

    up = pairwise(line, lambda i: LINE * partner_up(i // LINE) + i % LINE)
    down = pairwise(line, lambda i: LINE * partner_down(i // LINE) + i % LINE)
    third = up[:, LIFT_ROW, :, 128:].astype(F32).sum(axis=0)
    tops = tops + up[:, LIFT_ROW + 1, :, :128].astype(F32).sum(axis=0)
    top = pairwise(tops, lambda i: i ^ (2 * LINE))
    same = pl.pallas_call(
        pack_kernel,
        out_shape=shape_of((2, CHIPS, ROWS, RHS, LEAF), BF16),
        in_specs=[SMEM] + [VMEM] * 5,
        out_specs=VMEM,
        compiler_params=pltpu.CompilerParams(vmem_limit_bytes=4 * MIB),
        name="pack",
    )(me, line, up, down, third, top)
    other = pairwise(same, lambda i: i ^ 1)

    near = pl.pallas_call(
        own_kernel,
        out_shape=shape_of((BOXES, RHS, LEAF), F32),
        in_specs=[ANY] * 4,
        out_specs=VMEM,
        scratch_shapes=[
            pltpu.SMEM((8, 128), F32),
            pltpu.VMEM((BOXES, RHS, LEAF), BF16),
            pltpu.VMEM((BOXES, LEAF, LEAF), BF16),
            pltpu.SemaphoreType.DMA((6,)),
        ],
        compiler_params=pltpu.CompilerParams(vmem_limit_bytes=8 * MIB),
        name="own",
    )(weight, same, off(vectors), off(near_tiles))

    return pl.pallas_call(
        final_kernel,
        out_shape=shape_of((BOXES, RHS, LEAF), F32),
        in_specs=[ANY] * 4 + [VMEM] * 6,
        out_specs=ANY,
        scratch_shapes=[
            pltpu.VMEM((CORES, 2, CHIPS, ROWS, RHS, LEAF), BF16),
            pltpu.SMEM((BOXES, 128), I32),
            pltpu.SMEM((8, 128), F32),
            pltpu.VMEM((BOXES, RHS, LEAF), F32),
            pltpu.SemaphoreType.DMA((4,)),
            pltpu.SemaphoreType.DMA((2,)),
        ],
        compiler_params=pltpu.CompilerParams(vmem_limit_bytes=16 * MIB),
        name="final",
    )(place, weight, same, other, near, tiles, basis, transfer, coupling, level)


def solution(mesh):
    placed = (
        P("pts", None, None),
        P("pts", None, None),
        P("pts", None, None),
        P("pts", None, None),
        P("pts", None, None, None),
        P("pts", None),
        P("pts", None),
        P("pts"),
        P("pts", None),
        P("pts", None, None, None),
        P("pts", None, None, None),
    )
    return jax.shard_map(
        per_device, mesh=mesh, in_specs=placed, out_specs=P("pts", None, None), check_vma=False
    )
```

```python
import jax
import jax.numpy as jnp
from jax import lax
from jax.experimental import pallas as pl
from jax.experimental.pallas import tpu as pltpu
from jax.sharding import PartitionSpec as P

LEAF = 256
RANK = 64
RHS = 8
NEAR = 4
FAR = 6
UP = 5
BOXES = 16
LINE = 8
CHIPS = 4
CORES = 2
PER_ROW = LEAF // RANK
Q_ROW = BOXES
LIFT_ROW = Q_ROW + BOXES // PER_ROW
ROWS = LIFT_ROW + 2
Z_ROWS = CHIPS * LIFT_ROW + 1
ALL_ROWS = CHIPS * (ROWS + LIFT_ROW)
MIB = 1024 * 1024

F32 = jnp.float32
BF16 = jnp.bfloat16
I32 = jnp.int32
VMEM = pl.BlockSpec(memory_space=pltpu.VMEM)
SMEM = pl.BlockSpec(memory_space=pltpu.SMEM)
ANY = pl.BlockSpec(memory_space=pl.ANY)


def nt(a, b):
    return lax.dot_general(a, b, (((1,), (1,)), ((), ())), preferred_element_type=F32)


def nn(a, b):
    return lax.dot_general(a, b, (((1,), (0,)), ((), ())), preferred_element_type=F32)


def iota(shape, dim):
    return lax.broadcasted_iota(I32, shape, dim)


def partner_up(line):
    return line ^ 1


def partner_down(line):
    return ((line + 1) ^ 1) - 1


def front_kernel(
    me_ref,
    near_any,
    far_any,
    count_any,
    scale_any,
    vectors_any,
    basis_any,
    transfer_any,
    up_any,
    block_ref,
    place_ref,
    weight_ref,
    near,
    far,
    count,
    scale,
    vectors,
    basis,
    transfer,
    up,
    sems,
):
    pairs = (
        (vectors_any, vectors),
        (basis_any, basis),
        (transfer_any, transfer),
        (up_any, up),
        (near_any, near),
        (far_any, far),
        (count_any, count),
        (scale_any, scale),
    )
    copies = [pltpu.make_async_copy(a, b, sems.at[i]) for i, (a, b) in enumerate(pairs)]
    for copy in copies[4:] + copies[:4]:
        copy.start()
    for copy in copies[4:]:
        copy.wait()
    me = me_ref[0]
    line, home, core = me >> 3, (me >> 1) & 3, me & 1
    place_ref[...] = jnp.full((BOXES, 128), me, I32)
    for first, ref in ((0, near), (8, far)):
        box = ref[...]
        apart = ((box >> 4) & 1) ^ core
        beside = ((box >> 7) != line).astype(I32)
        chip = ((box >> 5) & 3) ^ home
        start = jnp.where(beside == 1, CHIPS * ROWS + LIFT_ROW * chip, ROWS * chip)
        place = (apart << 12) | (start << 4) | (box & 15)
        place_ref[first : first + box.shape[0], 0:BOXES] = place
    used = iota((NEAR, BOXES), 0) < jnp.broadcast_to(count[...].reshape(1, BOXES), (NEAR, BOXES))
    weight_ref[0:NEAR, 0:BOXES] = jnp.where(used, scale[...], 0.0)
    copies[0].wait()
    copies[1].wait()
    coefficients = [nt(vectors[b], basis[b]).astype(BF16) for b in range(BOXES)]
    copies[2].wait()
    joined = jnp.concatenate([q.astype(F32) for q in coefficients], axis=1).astype(BF16)
    total = nn(joined, transfer[...].reshape(BOXES * RANK, RANK)).astype(BF16)
    copies[3].wait()
    lifted = [nn(total, up[0, k].astype(BF16)) for k in range(UP)]
    nothing = jnp.zeros((RHS, RANK), F32)
    block_ref[:BOXES] = vectors[...]

    def put(row, pieces):
        block_ref[row] = jnp.concatenate(pieces, axis=1).astype(BF16)

    for j in range(PER_ROW):
        put(Q_ROW + j, [coefficients[PER_ROW * g + j].astype(F32) for g in range(PER_ROW)])
    put(LIFT_ROW, lifted[:4])
    put(LIFT_ROW + 1, [lifted[4], nothing, nothing, nothing])


def join_kernel(ready_any, own_ref, first_ref, second_ref, third_ref, line_ref, z_ref):
    refs = (own_ref, first_ref, second_ref, third_ref)
    for k, ref in enumerate(refs):
        line_ref[k * ROWS : (k + 1) * ROWS] = ref[...]
        z_ref[k * LIFT_ROW : (k + 1) * LIFT_ROW] = ref[:LIFT_ROW]
    sums = [
        sum(ref[row, :, lanes].astype(F32) for ref in refs)
        for row, lanes in ((LIFT_ROW, slice(128, LEAF)), (LIFT_ROW + 1, slice(0, 128)))
    ]
    z_ref[CHIPS * LIFT_ROW] = jnp.concatenate(sums, axis=1).astype(BF16)


def pack_kernel(me_ref, line_ref, up_ref, down_ref, top, out_ref):
    me = me_ref[0]
    home, core = me & 7, me & 1
    prev_is_up = ((me >> 3) & 1) == 1
    out_ref[: CHIPS * ROWS] = line_ref[...]
    for k in range(CHIPS):
        use_prev = (home ^ (2 * k)) > home if k else core == 1
        use_up = use_prev == prev_is_up
        rows = slice(k * LIFT_ROW, (k + 1) * LIFT_ROW)
        first = CHIPS * ROWS + k * LIFT_ROW

        @pl.when(use_up)
        def _():
            out_ref[first : first + LIFT_ROW] = up_ref[rows]

        @pl.when(jnp.logical_not(use_up))
        def _():
            out_ref[first : first + LIFT_ROW] = down_ref[rows]

    low = iota((RHS, 128), 1) < RANK
    third = up_ref[CHIPS * LIFT_ROW, :, :128].astype(F32)
    mixed = jnp.where(low, line_ref[LIFT_ROW, :, 128:].astype(F32), third)
    out_ref[LIFT_ROW, :, 128:] = mixed.astype(BF16)
    out_ref[LIFT_ROW + 1, :, :128] = top[...].astype(BF16)


def own_kernel(weight_any, after_any, vectors_any, tiles_any, near_ref, weight, vectors, mine, sems):
    copies = [
        pltpu.make_async_copy(vectors_any, vectors, sems.at[4]),
        pltpu.make_async_copy(weight_any, weight, sems.at[5]),
    ]
    parts = [
        pltpu.make_async_copy(tiles_any.at[pl.ds(b, 4), 0], mine.at[pl.ds(b, 4)], sems.at[b // 4])
        for b in range(0, BOXES, 4)
    ]
    for copy in copies + parts:
        copy.start()
    for copy in copies:
        copy.wait()
    for first in range(0, BOXES, 4):
        parts[first // 4].wait()
        products = [nt(vectors[b], mine[b]) for b in range(first, first + 4)]
        for b in range(first, first + 4):
            near_ref[b] = weight[0, b] * products[b - first]


def stage_kernel(
    after_any,
    tiles_any,
    basis_any,
    transfer_any,
    coupling_any,
    level_any,
    tiles_ref,
    basis_ref,
    transfer_ref,
    coupling_ref,
    level_ref,
    ready_ref,
    sems,
):
    pairs = (
        (tiles_any.at[:, pl.ds(1, NEAR - 1)], tiles_ref),
        (coupling_any, coupling_ref),
        (transfer_any, transfer_ref),
        (basis_any, basis_ref),
        (level_any, level_ref),
    )
    copies = [pltpu.make_async_copy(a, b, sems.at[i]) for i, (a, b) in enumerate(pairs)]
    for copy in copies:
        copy.start()
    ready_ref[...] = jnp.zeros((8, 128), F32)
    for copy in copies:
        copy.wait()


def final_kernel(
    place_any,
    weight_any,
    same_any,
    other_any,
    near,
    tiles,
    basis,
    transfer,
    coupling,
    level,
    out_any,
    window,
    place,
    weight,
    out,
    sems,
    out_sems,
):
    pairs = (
        (place_any, place),
        (weight_any, weight),
        (same_any, window.at[0]),
        (other_any, window.at[1]),
    )
    copies = [pltpu.make_async_copy(a, b, sems.at[i]) for i, (a, b) in enumerate(pairs)]
    for copy in copies:
        copy.start()
    for copy in copies:
        copy.wait()

    def entry(row, b):
        at = place[row, b]
        return at >> 12, (at >> 4) & 255, at & 15

    def vectors(row, b):
        half, start, box = entry(row, b)
        return window[half, start + box]

    def levels(half, k, level):
        row, lane = LIFT_ROW + level // PER_ROW, level % PER_ROW * RANK
        return window[half, k * ROWS + row].astype(F32)[:, lane : lane + RANK]

    for first in range(0, BOXES, 2):
        parts = [
            [nt(vectors(s, b), tiles[b, s - 1]) for s in range(1, NEAR)]
            for b in range(first, first + 2)
        ]
        for b in range(first, first + 2):
            total = near[b]
            for s in range(1, NEAR):
                total = total + weight[s, b] * parts[b - first][s - 1]
            out[b] = total

    groups = [
        levels(1, 0, 0),
        levels(0, 1, 1) + levels(1, 1, 1),
        levels(0, 2, 2) + levels(1, 2, 2) + levels(0, 3, 2) + levels(1, 3, 2),
        levels(0, 0, 3) + levels(1, 0, 3),
        levels(0, 0, 4) + levels(1, 0, 4),
    ]
    far_field = jnp.zeros((RHS, RANK), F32)
    for k in range(UP):
        far_field = far_field + nn(groups[k].astype(BF16), level[0, k].astype(BF16))
    far_field = far_field.astype(BF16)

    low = iota((RHS, 128), 1) < RANK

    def coefficient(row, b, odd):
        half, start, box = entry(row, b)
        lanes = pl.ds(pl.multiple_of((box >> 3) * 128, 128), 128)
        piece = window[half, start + Q_ROW + (box & 3), :, lanes].astype(F32)
        return pltpu.roll(piece, (((box >> 2) & 1) ^ odd) * RANK, 1)

    leaves = []
    for b in range(BOXES):
        halves = [coefficient(8 + s, b, s & 1) for s in range(FAR)]
        joined = jnp.concatenate(
            [jnp.where(low, halves[2 * i], halves[2 * i + 1]) for i in range(FAR // 2)], axis=1
        ).astype(BF16)
        leaves.append(nt(joined, coupling[b]))
    leaves = [(leaves[b] + nt(far_field, transfer[b])).astype(BF16) for b in range(BOXES)]
    outs = []
    for b in range(BOXES):
        out[b] = out[b] + nn(leaves[b], basis[b])
        if b % 8 == 7:
            rows = pl.ds(b - 7, 8)
            outs.append(
                pltpu.make_async_copy(out.at[rows], out_any.at[rows], out_sems.at[b // 8])
            )
            outs[-1].start()
    for copy in outs:
        copy.wait()


def pairwise(block, partner):
    count = lax.axis_size("pts")
    route = [(i, partner(i)) for i in range(count) if 0 <= partner(i) < count]
    return lax.ppermute(block, "pts", route)


def shape_of(shape, dtype):
    return jax.ShapeDtypeStruct(shape, dtype)


def per_device(
    vectors,
    leaf_basis,
    leaf_transfer,
    leaf_coupling,
    near_tiles,
    tile_scale,
    near_boxes,
    near_counts,
    far_boxes,
    level_up,
    level_coupling,
):
    me = lax.axis_index("pts").astype(I32).reshape(1)

    def off(x):
        return pltpu.with_memory_space_constraint(x, pltpu.HBM)

    block, place, weight = pl.pallas_call(
        front_kernel,
        out_shape=(
            shape_of((ROWS, RHS, LEAF), BF16),
            shape_of((BOXES, 128), I32),
            shape_of((8, 128), F32),
        ),
        in_specs=[SMEM] + [ANY] * 8,
        out_specs=(VMEM,) * 3,
        scratch_shapes=[
            pltpu.VMEM((NEAR, BOXES), I32),
            pltpu.VMEM((FAR, BOXES), I32),
            pltpu.VMEM((BOXES,), I32),
            pltpu.VMEM((NEAR, BOXES), F32),
            pltpu.VMEM((BOXES, RHS, LEAF), BF16),
            pltpu.VMEM((BOXES, RANK, LEAF), BF16),
            pltpu.VMEM((BOXES, RANK, RANK), BF16),
            pltpu.VMEM((1, UP, RANK, RANK), F32),
            pltpu.SemaphoreType.DMA((8,)),
        ],
        compiler_params=pltpu.CompilerParams(vmem_limit_bytes=8 * MIB),
        name="front",
    )(
        me,
        off(near_boxes.T),
        off(far_boxes.T),
        off(near_counts),
        off(tile_scale.T),
        off(vectors),
        off(leaf_basis),
        off(leaf_transfer),
        off(level_up),
    )

    tiles, basis, transfer, coupling, level, ready = pl.pallas_call(
        stage_kernel,
        out_shape=(
            pltpu.VMEM((BOXES, NEAR - 1, LEAF, LEAF), BF16),
            pltpu.VMEM((BOXES, RANK, LEAF), BF16),
            pltpu.VMEM((BOXES, RANK, RANK), BF16),
            pltpu.VMEM((BOXES, RANK, FAR * RANK), BF16),
            pltpu.VMEM((1, UP, RANK, RANK), F32),
            shape_of((8, 128), F32),
        ),
        in_specs=[ANY] * 6,
        out_specs=(ANY,) * 5 + (VMEM,),
        scratch_shapes=[pltpu.SemaphoreType.DMA((5,))],
        compiler_params=pltpu.CompilerParams(vmem_limit_bytes=4 * MIB),
        name="stage",
    )(
        block,
        off(near_tiles),
        off(leaf_basis),
        off(leaf_transfer),
        off(leaf_coupling),
        off(level_coupling),
    )

    first, third, second = [
        pairwise(block, lambda i, k=k: i ^ (CORES * k)) for k in (1, 3, 2)
    ]
    line, z_line = pl.pallas_call(
        join_kernel,
        out_shape=(
            shape_of((CHIPS * ROWS, RHS, LEAF), BF16),
            shape_of((Z_ROWS, RHS, LEAF), BF16),
        ),
        in_specs=[ANY] + [VMEM] * CHIPS,
        out_specs=(VMEM, VMEM),
        compiler_params=pltpu.CompilerParams(vmem_limit_bytes=4 * MIB),
        name="join",
    )(
        ready,
        block,
        first,
        second,
        third,
    )

    up = pairwise(z_line, lambda i: LINE * partner_up(i // LINE) + i % LINE)
    down = pairwise(z_line, lambda i: LINE * partner_down(i // LINE) + i % LINE)
    tops = z_line[-1, :, 128:].astype(F32) + up[-1, :, 128:].astype(F32)
    top = pairwise(tops, lambda i: i ^ (2 * LINE))
    same = pl.pallas_call(
        pack_kernel,
        out_shape=shape_of((ALL_ROWS, RHS, LEAF), BF16),
        in_specs=[SMEM] + [VMEM] * 4,
        out_specs=VMEM,
        compiler_params=pltpu.CompilerParams(vmem_limit_bytes=4 * MIB),
        name="pack",
    )(me, line, up, down, top)
    other = pairwise(same, lambda i: i ^ 1)

    near = pl.pallas_call(
        own_kernel,
        out_shape=shape_of((BOXES, RHS, LEAF), F32),
        in_specs=[ANY] * 4,
        out_specs=VMEM,
        scratch_shapes=[
            pltpu.SMEM((8, 128), F32),
            pltpu.VMEM((BOXES, RHS, LEAF), BF16),
            pltpu.VMEM((BOXES, LEAF, LEAF), BF16),
            pltpu.SemaphoreType.DMA((6,)),
        ],
        compiler_params=pltpu.CompilerParams(vmem_limit_bytes=8 * MIB),
        name="own",
    )(weight, same, off(vectors), off(near_tiles))

    return pl.pallas_call(
        final_kernel,
        out_shape=shape_of((BOXES, RHS, LEAF), F32),
        in_specs=[ANY] * 4 + [VMEM] * 6,
        out_specs=ANY,
        scratch_shapes=[
            pltpu.VMEM((CORES, ALL_ROWS, RHS, LEAF), BF16),
            pltpu.SMEM((BOXES, 128), I32),
            pltpu.SMEM((8, 128), F32),
            pltpu.VMEM((BOXES, RHS, LEAF), F32),
            pltpu.SemaphoreType.DMA((4,)),
            pltpu.SemaphoreType.DMA((2,)),
        ],
        compiler_params=pltpu.CompilerParams(vmem_limit_bytes=16 * MIB),
        name="final",
    )(place, weight, same, other, near, tiles, basis, transfer, coupling, level)


def solution(mesh):
    placed = (
        P("pts", None, None),
        P("pts", None, None),
        P("pts", None, None),
        P("pts", None, None),
        P("pts", None, None, None),
        P("pts", None),
        P("pts", None),
        P("pts"),
        P("pts", None),
        P("pts", None, None, None),
        P("pts", None, None, None),
    )
    return jax.shard_map(
        per_device, mesh=mesh, in_specs=placed, out_specs=P("pts", None, None), check_vma=False
    )
```

```python
import jax
import jax.numpy as jnp
from jax import lax
from jax.experimental import pallas as pl
from jax.experimental.pallas import tpu as pltpu
from jax.sharding import PartitionSpec as P

LEAF = 256
RANK = 64
RHS = 8
NEAR = 4
FAR = 6
UP = 5
BOXES = 16
LINE = 8
CHIPS = 4
CORES = 2
PER_ROW = LEAF // RANK
Q_ROW = BOXES
LIFT_ROW = Q_ROW + BOXES // PER_ROW
ROWS = LIFT_ROW + 1
Z_ROWS = CHIPS * LIFT_ROW + 1
SUM_ROW = CHIPS * ROWS
ALL_ROWS = SUM_ROW + 1 + CHIPS * LIFT_ROW
MIB = 1024 * 1024

F32 = jnp.float32
BF16 = jnp.bfloat16
I32 = jnp.int32
VMEM = pl.BlockSpec(memory_space=pltpu.VMEM)
SMEM = pl.BlockSpec(memory_space=pltpu.SMEM)
ANY = pl.BlockSpec(memory_space=pl.ANY)


def nt(a, b):
    return lax.dot_general(a, b, (((1,), (1,)), ((), ())), preferred_element_type=F32)


def nn(a, b):
    return lax.dot_general(a, b, (((1,), (0,)), ((), ())), preferred_element_type=F32)


def iota(shape, dim):
    return lax.broadcasted_iota(I32, shape, dim)


def partner_up(line):
    return line ^ 1


def partner_down(line):
    return ((line + 1) ^ 1) - 1


def front_kernel(
    me_ref,
    near_any,
    far_any,
    count_any,
    scale_any,
    vectors_any,
    basis_any,
    transfer_any,
    up_any,
    block_ref,
    place_ref,
    weight_ref,
    zero_ref,
    near,
    far,
    count,
    scale,
    vectors,
    basis,
    transfer,
    up,
    sems,
):
    pairs = (
        (vectors_any, vectors),
        (basis_any, basis),
        (transfer_any, transfer),
        (up_any, up),
        (near_any, near),
        (far_any, far),
        (count_any, count),
        (scale_any, scale),
    )
    copies = [pltpu.make_async_copy(a, b, sems.at[i]) for i, (a, b) in enumerate(pairs)]
    for copy in copies[4:] + copies[:4]:
        copy.start()
    for copy in copies[4:]:
        copy.wait()
    me = me_ref[0]
    line, home, core = me >> 3, (me >> 1) & 3, me & 1
    place_ref[...] = jnp.full((BOXES, 128), me, I32)
    for first, ref in ((0, near), (8, far)):
        box = ref[...]
        apart = ((box >> 4) & 1) ^ core
        beside = ((box >> 7) != line).astype(I32)
        chip = ((box >> 5) & 3) ^ home
        start = jnp.where(beside == 1, SUM_ROW + 1 + LIFT_ROW * chip, ROWS * chip)
        place = (apart << 12) | (start << 4) | (box & 15)
        place_ref[first : first + box.shape[0], 0:BOXES] = place
    used = iota((NEAR, BOXES), 0) < jnp.broadcast_to(count[...].reshape(1, BOXES), (NEAR, BOXES))
    weight_ref[0:NEAR, 0:BOXES] = jnp.where(used, scale[...], 0.0)
    copies[0].wait()
    copies[1].wait()
    coefficients = [nt(vectors[b], basis[b]).astype(BF16) for b in range(BOXES)]
    copies[2].wait()
    joined = jnp.concatenate([q.astype(F32) for q in coefficients], axis=1).astype(BF16)
    total = nn(joined, transfer[...].reshape(BOXES * RANK, RANK)).astype(BF16)
    copies[3].wait()
    lifted = [nn(total, up[0, k].astype(BF16)) for k in range(UP)]
    nothing = jnp.zeros((RHS, RANK), F32)
    block_ref[:BOXES] = vectors[...]

    def put(row, pieces):
        block_ref[row] = jnp.concatenate(pieces, axis=1).astype(BF16)

    for j in range(PER_ROW):
        put(Q_ROW + j, [coefficients[PER_ROW * g + j].astype(F32) for g in range(PER_ROW)])
    put(LIFT_ROW, lifted[1:])
    zero_ref[...] = jnp.concatenate([lifted[0], nothing], axis=1)


def join_kernel(ready_any, own_ref, first_ref, second_ref, third_ref, line_ref, z_ref):
    refs = (own_ref, first_ref, second_ref, third_ref)
    for k, ref in enumerate(refs):
        line_ref[k * ROWS : (k + 1) * ROWS] = ref[...]
        z_ref[k * LIFT_ROW : (k + 1) * LIFT_ROW] = ref[:LIFT_ROW]
    sums = sum(ref[LIFT_ROW, :, 128:].astype(F32) for ref in refs)
    z_ref[CHIPS * LIFT_ROW] = jnp.concatenate([sums, jnp.zeros_like(sums)], axis=1).astype(BF16)


def pack_kernel(me_ref, line_ref, up_ref, down_ref, top, zero, out_ref):
    me = me_ref[0]
    home, core = me & 7, me & 1
    prev_is_up = ((me >> 3) & 1) == 1
    out_ref[:SUM_ROW] = line_ref[...]
    for k in range(CHIPS):
        use_prev = (home ^ (2 * k)) > home if k else core == 1
        use_up = use_prev == prev_is_up
        rows = slice(k * LIFT_ROW, (k + 1) * LIFT_ROW)
        first = SUM_ROW + 1 + k * LIFT_ROW

        @pl.when(use_up)
        def _():
            out_ref[first : first + LIFT_ROW] = up_ref[rows]

        @pl.when(jnp.logical_not(use_up))
        def _():
            out_ref[first : first + LIFT_ROW] = down_ref[rows]

    low = iota((RHS, 128), 1) < RANK
    sums = jnp.where(low, up_ref[CHIPS * LIFT_ROW, :, :128].astype(F32), top[...])
    out_ref[SUM_ROW] = jnp.concatenate([sums, zero[...]], axis=1).astype(BF16)


def own_kernel(weight_any, after_any, vectors_any, tiles_any, near_ref, weight, vectors, mine, sems):
    copies = [
        pltpu.make_async_copy(vectors_any, vectors, sems.at[4]),
        pltpu.make_async_copy(weight_any, weight, sems.at[5]),
    ]
    parts = [
        pltpu.make_async_copy(tiles_any.at[pl.ds(b, 4), 0], mine.at[pl.ds(b, 4)], sems.at[b // 4])
        for b in range(0, BOXES, 4)
    ]
    for copy in copies + parts:
        copy.start()
    for copy in copies:
        copy.wait()
    for first in range(0, BOXES, 4):
        parts[first // 4].wait()
        products = [nt(vectors[b], mine[b]) for b in range(first, first + 4)]
        for b in range(first, first + 4):
            near_ref[b] = weight[0, b] * products[b - first]


def stage_kernel(
    after_any,
    tiles_any,
    basis_any,
    transfer_any,
    coupling_any,
    level_any,
    tiles_ref,
    basis_ref,
    transfer_ref,
    coupling_ref,
    level_ref,
    ready_ref,
    sems,
):
    pairs = (
        (tiles_any.at[:, pl.ds(1, NEAR - 1)], tiles_ref),
        (coupling_any, coupling_ref),
        (transfer_any, transfer_ref),
        (basis_any, basis_ref),
        (level_any, level_ref),
    )
    copies = [pltpu.make_async_copy(a, b, sems.at[i]) for i, (a, b) in enumerate(pairs)]
    for copy in copies:
        copy.start()
    ready_ref[...] = jnp.zeros((8, 128), F32)
    for copy in copies:
        copy.wait()


def final_kernel(
    place_any,
    weight_any,
    same_any,
    other_any,
    near,
    tiles,
    basis,
    transfer,
    coupling,
    level,
    out_any,
    window,
    place,
    weight,
    out,
    sems,
    out_sems,
):
    pairs = (
        (place_any, place),
        (weight_any, weight),
        (same_any, window.at[0]),
        (other_any, window.at[1]),
    )
    copies = [pltpu.make_async_copy(a, b, sems.at[i]) for i, (a, b) in enumerate(pairs)]
    for copy in copies:
        copy.start()
    for copy in copies:
        copy.wait()

    def entry(row, b):
        at = place[row, b]
        return at >> 12, (at >> 4) & 255, at & 15

    def vectors(row, b):
        half, start, box = entry(row, b)
        return window[half, start + box]

    def levels(half, row, lane):
        return window[half, row].astype(F32)[:, lane * RANK : (lane + 1) * RANK]

    def lifts(half, k, level):
        return levels(half, k * ROWS + LIFT_ROW, level - 1)

    for first in range(0, BOXES, 4):
        parts = [
            [nt(vectors(s, b), tiles[b, s - 1]) for s in range(1, NEAR)]
            for b in range(first, first + 4)
        ]
        for b in range(first, first + 4):
            total = near[b]
            for s in range(1, NEAR):
                total = total + weight[s, b] * parts[b - first][s - 1]
            out[b] = total

    groups = [
        levels(1, SUM_ROW, 2),
        lifts(0, 1, 1) + lifts(1, 1, 1),
        lifts(0, 2, 2) + lifts(1, 2, 2) + lifts(0, 3, 2) + lifts(1, 3, 2),
        levels(0, SUM_ROW, 0) + levels(1, SUM_ROW, 0),
        levels(0, SUM_ROW, 1) + levels(1, SUM_ROW, 1),
    ]
    far_field = jnp.zeros((RHS, RANK), F32)
    for k in range(UP):
        far_field = far_field + nn(groups[k].astype(BF16), level[0, k].astype(BF16))
    far_field = far_field.astype(BF16)

    low = iota((RHS, 128), 1) < RANK

    def coefficient(row, b, odd):
        half, start, box = entry(row, b)
        lanes = pl.ds(pl.multiple_of((box >> 3) * 128, 128), 128)
        piece = window[half, start + Q_ROW + (box & 3), :, lanes].astype(F32)
        return pltpu.roll(piece, (((box >> 2) & 1) ^ odd) * RANK, 1)

    leaves = []
    for b in range(BOXES):
        halves = [coefficient(8 + s, b, s & 1) for s in range(FAR)]
        joined = jnp.concatenate(
            [jnp.where(low, halves[2 * i], halves[2 * i + 1]) for i in range(FAR // 2)], axis=1
        ).astype(BF16)
        leaves.append(nt(joined, coupling[b]))
    leaves = [(leaves[b] + nt(far_field, transfer[b])).astype(BF16) for b in range(BOXES)]
    outs = []
    for b in range(BOXES):
        out[b] = out[b] + nn(leaves[b], basis[b])
        if b % 4 == 3:
            rows = pl.ds(b - 3, 4)
            outs.append(
                pltpu.make_async_copy(out.at[rows], out_any.at[rows], out_sems.at[b // 4])
            )
            outs[-1].start()
    for copy in outs:
        copy.wait()


def pairwise(block, partner):
    count = lax.axis_size("pts")
    route = [(i, partner(i)) for i in range(count) if 0 <= partner(i) < count]
    return lax.ppermute(block, "pts", route)


def shape_of(shape, dtype):
    return jax.ShapeDtypeStruct(shape, dtype)


def per_device(
    vectors,
    leaf_basis,
    leaf_transfer,
    leaf_coupling,
    near_tiles,
    tile_scale,
    near_boxes,
    near_counts,
    far_boxes,
    level_up,
    level_coupling,
):
    me = lax.axis_index("pts").astype(I32).reshape(1)

    def off(x):
        return pltpu.with_memory_space_constraint(x, pltpu.HBM)

    block, place, weight, zero = pl.pallas_call(
        front_kernel,
        out_shape=(
            shape_of((ROWS, RHS, LEAF), BF16),
            shape_of((BOXES, 128), I32),
            shape_of((8, 128), F32),
            shape_of((RHS, 128), F32),
        ),
        in_specs=[SMEM] + [ANY] * 8,
        out_specs=(VMEM,) * 4,
        scratch_shapes=[
            pltpu.VMEM((NEAR, BOXES), I32),
            pltpu.VMEM((FAR, BOXES), I32),
            pltpu.VMEM((BOXES,), I32),
            pltpu.VMEM((NEAR, BOXES), F32),
            pltpu.VMEM((BOXES, RHS, LEAF), BF16),
            pltpu.VMEM((BOXES, RANK, LEAF), BF16),
            pltpu.VMEM((BOXES, RANK, RANK), BF16),
            pltpu.VMEM((1, UP, RANK, RANK), F32),
            pltpu.SemaphoreType.DMA((8,)),
        ],
        compiler_params=pltpu.CompilerParams(vmem_limit_bytes=8 * MIB),
        name="front",
    )(
        me,
        off(near_boxes.T),
        off(far_boxes.T),
        off(near_counts),
        off(tile_scale.T),
        off(vectors),
        off(leaf_basis),
        off(leaf_transfer),
        off(level_up),
    )

    tiles, basis, transfer, coupling, level, ready = pl.pallas_call(
        stage_kernel,
        out_shape=(
            pltpu.VMEM((BOXES, NEAR - 1, LEAF, LEAF), BF16),
            pltpu.VMEM((BOXES, RANK, LEAF), BF16),
            pltpu.VMEM((BOXES, RANK, RANK), BF16),
            pltpu.VMEM((BOXES, RANK, FAR * RANK), BF16),
            pltpu.VMEM((1, UP, RANK, RANK), F32),
            shape_of((8, 128), F32),
        ),
        in_specs=[ANY] * 6,
        out_specs=(ANY,) * 5 + (VMEM,),
        scratch_shapes=[pltpu.SemaphoreType.DMA((5,))],
        compiler_params=pltpu.CompilerParams(vmem_limit_bytes=4 * MIB),
        name="stage",
    )(
        block,
        off(near_tiles),
        off(leaf_basis),
        off(leaf_transfer),
        off(leaf_coupling),
        off(level_coupling),
    )

    first, third, second = [
        pairwise(block, lambda i, k=k: i ^ (CORES * k)) for k in (1, 3, 2)
    ]
    line, z_line = pl.pallas_call(
        join_kernel,
        out_shape=(
            shape_of((CHIPS * ROWS, RHS, LEAF), BF16),
            shape_of((Z_ROWS, RHS, LEAF), BF16),
        ),
        in_specs=[ANY] + [VMEM] * CHIPS,
        out_specs=(VMEM, VMEM),
        compiler_params=pltpu.CompilerParams(vmem_limit_bytes=4 * MIB),
        name="join",
    )(
        ready,
        block,
        first,
        second,
        third,
    )

    up = pairwise(z_line, lambda i: LINE * partner_up(i // LINE) + i % LINE)
    down = pairwise(z_line, lambda i: LINE * partner_down(i // LINE) + i % LINE)
    tops = z_line[-1, :, :128].astype(F32) + up[-1, :, :128].astype(F32)
    top = pairwise(tops, lambda i: i ^ (2 * LINE))
    same = pl.pallas_call(
        pack_kernel,
        out_shape=shape_of((ALL_ROWS, RHS, LEAF), BF16),
        in_specs=[SMEM] + [VMEM] * 5,
        out_specs=VMEM,
        compiler_params=pltpu.CompilerParams(vmem_limit_bytes=4 * MIB),
        name="pack",
    )(me, line, up, down, top, zero)
    other = pairwise(same, lambda i: i ^ 1)

    near = pl.pallas_call(
        own_kernel,
        out_shape=shape_of((BOXES, RHS, LEAF), F32),
        in_specs=[ANY] * 4,
        out_specs=VMEM,
        scratch_shapes=[
            pltpu.SMEM((8, 128), F32),
            pltpu.VMEM((BOXES, RHS, LEAF), BF16),
            pltpu.VMEM((BOXES, LEAF, LEAF), BF16),
            pltpu.SemaphoreType.DMA((6,)),
        ],
        compiler_params=pltpu.CompilerParams(vmem_limit_bytes=8 * MIB),
        name="own",
    )(weight, same, off(vectors), off(near_tiles))

    return pl.pallas_call(
        final_kernel,
        out_shape=shape_of((BOXES, RHS, LEAF), F32),
        in_specs=[ANY] * 4 + [VMEM] * 6,
        out_specs=ANY,
        scratch_shapes=[
            pltpu.VMEM((CORES, ALL_ROWS, RHS, LEAF), BF16),
            pltpu.SMEM((BOXES, 128), I32),
            pltpu.SMEM((8, 128), F32),
            pltpu.VMEM((BOXES, RHS, LEAF), F32),
            pltpu.SemaphoreType.DMA((4,)),
            pltpu.SemaphoreType.DMA((4,)),
        ],
        compiler_params=pltpu.CompilerParams(vmem_limit_bytes=16 * MIB),
        name="final",
    )(place, weight, same, other, near, tiles, basis, transfer, coupling, level)


def solution(mesh):
    placed = (
        P("pts", None, None),
        P("pts", None, None),
        P("pts", None, None),
        P("pts", None, None),
        P("pts", None, None, None),
        P("pts", None),
        P("pts", None),
        P("pts"),
        P("pts", None),
        P("pts", None, None, None),
        P("pts", None, None, None),
    )
    return jax.shard_map(
        per_device, mesh=mesh, in_specs=placed, out_specs=P("pts", None, None), check_vma=False
    )
```
